32 devices in a mesh: seq: 8 (over y, x, core), chan: 4 (over z).
Axes of the slice: x: 2, y: 2, z: 4, core: 2. Of those that a mesh axis runs over, the one named last changes fastest.
Arguments:
- hyena_query: bfloat16 [2048, 8192], P('seq', 'chan'), may hold values from -6 to 6
- hyena_key: bfloat16 [2048, 8192], P('seq', 'chan'), may hold values from -6 to 6
- hyena_value: bfloat16 [2048, 8192], P('seq', 'chan'), may hold values from -6 to 6
- bias: float32 [8192], P('chan'), may hold values from 0.5 to 1.5
- groups: int32 [8192], P('chan'), may hold values from 0 to 511
- filters: float32 [512, 2048], P('chan', 'seq'), may hold values from -1.5 to 1.5
- att_queries: bfloat16 [2048, 8192], P('seq', 'chan'), may hold values from -45 to 45
- att_keys: bfloat16 [2048, 8192], P('seq', 'chan'), may hold values from -5 to 5
- block_mask: int32 [16, 16], P('seq'), may hold values from 0 to 1, as said below
Outputs:
- hyena_out: bfloat16 [2048, 8192], P('seq', 'chan')
- attn_out: bfloat16 [2048, 8192], P('seq', 'chan')
The draws below stay inside these ranges and needn't reach their ends.
Inputs may be any that keep to these rules, and one draw needn't show every extreme that they name: block_mask[i, i] = 1 and block_mask[i, j] = 0 for j > i.
All inputs are finite; a program needn't handle non-finite values.
Results may differ from the reference program's by a relative error of at most 0.014.
Values may be sent and summed in bfloat16 or wider, within the bound.
A program may use at most 128 MiB of HBM per device.

```python
import math
import jax
import jax.numpy as jnp
from jax import lax

D = 8192
HD = 128
HEADS = 64
FGROUPS = 512
ABLK = 128
TOKENS = 2048
NBLK = 16
N_CHAN = 4


def draw_filters(key, part):
    base = jax.random.fold_in(key, 3)
    key_noise, key_rate = jax.random.split(base)
    lengths = jnp.exp(jax.random.uniform(key_rate, (FGROUPS, 1), jnp.float32, math.log(40.0), math.log(4.0 * TOKENS)))
    noise = jnp.clip(jax.random.normal(key_noise, (FGROUPS, TOKENS), jnp.float32), -5.0, 5.0)
    effective = jnp.minimum(lengths, 1.0 * TOKENS)
    amplitude = jnp.sqrt(2.0 / effective)
    lags = jnp.arange(TOKENS, dtype=jnp.float32)[None, :]
    return noise * amplitude * jnp.exp(-lags / lengths)


def shared_keys(key):
    base = jax.random.fold_in(key, 7)
    key_main = jax.random.fold_in(base, 0)
    keys = jnp.clip(jax.random.normal(key_main, (TOKENS, D), jnp.float32), -4.0, 4.0)
    return keys


def draw_att_keys(key, part):
    return shared_keys(key).astype(jnp.bfloat16)


def draw_att_queries(key, part):
    key_query = jax.random.fold_in(key, 11)
    key_main = jax.random.fold_in(key_query, 0)
    queries = jnp.clip(jax.random.normal(key_main, (TOKENS, D), jnp.float32), -4.0, 4.0)
    return queries.astype(jnp.bfloat16)


def draw_block_mask(key, part):
    base = jax.random.fold_in(key, 5)
    coins = jax.random.randint(base, (NBLK, NBLK), 0, 2)
    row_index = jnp.arange(NBLK, dtype=jnp.int32)[:, None]
    col_index = jnp.arange(NBLK, dtype=jnp.int32)[None, :]
    return jnp.where(col_index < row_index, coins, jnp.where(col_index == row_index, 1, 0)).astype(jnp.int32)


def plant(entries, key, least, top_value):
    dims = entries.shape
    index_at = [jax.random.randint(jax.random.fold_in(key, axis), (), 0, dims[axis]) for axis in range(len(dims))]
    entries = entries.at[tuple(index_at)].set(least)
    longest = dims.index(max(dims))
    index_at[longest] = (index_at[longest] + 1) % dims[longest]
    return entries.at[tuple(index_at)].set(top_value)


def block_levels(stream_key, extent, cuts, low, top_value):
    loudness = 1.0
    for position, parts in cuts:
        draws = jax.random.uniform(jax.random.fold_in(jax.random.fold_in(stream_key, 6), position), (parts,), jnp.float32, low / len(cuts), top_value / len(cuts))
        loudness = loudness * jnp.repeat(jnp.exp(draws), extent[position] // parts).reshape((-1,) + (1,) * (len(extent) - 1 - position))
    return loudness


def scatter_about(key, dims, spread, limit, cuts=(), held_as=jnp.bfloat16):
    gain = block_levels(key, dims, cuts, -0.22, 0.18) if cuts else 1.0
    result = jax.random.normal(key, dims, jnp.float32) * spread * gain
    return jnp.minimum(jnp.maximum(result, -limit), limit).astype(held_as)


def setup_inputs(seed: int = 0) -> dict:
    arg_keys = jax.random.split(jax.random.key(seed), 10)
    hyena_query = scatter_about(arg_keys[0], (TOKENS, D), 1.0, 6.0, ((0, 8), (1, 4)))
    hyena_key = scatter_about(arg_keys[1], (TOKENS, D), 1.0, 6.0, ((0, 8), (1, 4)))
    hyena_value = scatter_about(arg_keys[2], (TOKENS, D), 1.0, 6.0, ((0, 8), (1, 4)))
    bias = jnp.clip(0.5 + 1.0 * jax.random.uniform(arg_keys[3], (D,), jnp.float32) ** block_levels(arg_keys[3], (D,), ((0, 4),), -0.2, 0.2), 0.5, 1.5)
    groups = plant(jax.random.randint(arg_keys[4], (D,), 0, FGROUPS), jax.random.fold_in(arg_keys[4], 1), 0, FGROUPS - 1).astype(jnp.int32)
    filters = draw_filters(jax.random.fold_in(arg_keys[9], 71), 0)
    att_queries = draw_att_queries(jax.random.fold_in(arg_keys[9], 71), 0)
    att_keys = draw_att_keys(jax.random.fold_in(arg_keys[9], 71), 0)
    block_mask = draw_block_mask(jax.random.fold_in(arg_keys[9], 71), 0)
    return dict(hyena_query=hyena_query, hyena_key=hyena_key, hyena_value=hyena_value, bias=bias, groups=groups, filters=filters, att_queries=att_queries, att_keys=att_keys, block_mask=block_mask)


def reference(hyena_query, hyena_key, hyena_value, bias, groups, filters, att_queries, att_keys, block_mask):
    mixed = (hyena_key.astype(jnp.float32) * hyena_value.astype(jnp.float32)).astype(jnp.bfloat16)
    values = mixed.astype(jnp.float32)
    width = D // N_CHAN
    blocks = values.reshape(TOKENS, N_CHAN, width).transpose(1, 0, 2)
    group_blocks = groups.reshape(N_CHAN, width)

    def convolve(pair):
        signal, chosen = pair
        kernel = filters[chosen].T
        spectrum = jnp.fft.rfft(signal, n=2 * TOKENS, axis=0) * jnp.fft.rfft(kernel, n=2 * TOKENS, axis=0)
        return jnp.fft.irfft(spectrum, n=2 * TOKENS, axis=0)[:TOKENS]

    conv = lax.map(convolve, (blocks, group_blocks)).transpose(1, 0, 2).reshape(TOKENS, D)
    hyena_out = (hyena_query.astype(jnp.float32) * (conv + bias[None, :] * values)).astype(jnp.bfloat16)

    positions = jnp.arange(TOKENS, dtype=jnp.int32)
    block_ids = positions // ABLK
    allowed = (block_mask[block_ids[:, None], block_ids[None, :]] == 1) & (positions[None, :] <= positions[:, None])
    queries = att_queries.reshape(TOKENS, HEADS, HD).transpose(1, 0, 2)
    keys = att_keys.reshape(TOKENS, HEADS, HD).transpose(1, 0, 2)
    heads_values = hyena_out.reshape(TOKENS, HEADS, HD).transpose(1, 0, 2)

    def one_head(triple):
        query_head, key_head, value_head = triple
        scores = jnp.dot(query_head, key_head.T, preferred_element_type=jnp.float32) * (HD ** -0.5)
        masked = jnp.where(allowed, scores, -jnp.inf)
        largest = jnp.max(masked, axis=-1, keepdims=True)
        weights = jnp.where(allowed, jnp.exp(masked - largest), 0.0)
        totals = jnp.sum(weights, axis=-1, keepdims=True)
        return jnp.dot(weights.astype(jnp.bfloat16), value_head, preferred_element_type=jnp.float32) / totals

    attended = lax.map(one_head, (queries, keys, heads_values))
    attn_out = attended.transpose(1, 0, 2).reshape(TOKENS, D).astype(jnp.bfloat16)
    return hyena_out, attn_out
```

```python
import functools
import math

import jax
import jax.numpy as jnp
import ml_dtypes
import numpy as np
from jax import lax
from jax.experimental import pallas as pl
from jax.experimental.pallas import tpu as pltpu
from jax.sharding import PartitionSpec as P

HD = 128
ABLK = 128


highest = lax.Precision.HIGHEST


def swapped(value, axis, stride):
    mask = 2**stride
    pairs = [(source, source ^ mask) for source in range(lax.axis_size(axis))]
    return lax.ppermute(value, axis, pairs)


def shortened(x):

    def short(part):
        return part.astype(jnp.bfloat16) if part.dtype == jnp.float32 else part

    return jax.tree.map(short, x)


def unit_angle(numer, denom):
    return 2.0 * math.pi / denom * numer.astype(jnp.float32)


def twist(real_part, imag_part, cosine, sine):
    return (real_part * cosine - imag_part * sine, real_part * sine + imag_part * cosine)


def expand_pair(signal, device, rows_dev, length):
    positions = device * rows_dev + jnp.arange(rows_dev, dtype=jnp.int32)
    angles = math.pi / length * positions.astype(jnp.float32)
    values = signal.astype(jnp.float32)
    cosine = jnp.cos(angles)[:, None]
    sine = jnp.sin(angles)[:, None]
    real_part = jnp.stack([values, values * cosine])
    imag_part = jnp.stack([jnp.zeros_like(values), -values * sine])
    return (real_part, imag_part)


def section_twiddle(device, level, rows_dev, sign):
    inner = device % (1 << level) * rows_dev + jnp.arange(rows_dev, dtype=jnp.int32)
    angles = unit_angle(inner, rows_dev << level + 1)
    return (jnp.cos(angles)[:, None], sign * jnp.sin(angles)[:, None])


def forward_section(current, partner, device, level, rows_dev):
    cosine, sine = section_twiddle(device, level, rows_dev, -1.0)
    upper = device >> level & 1 == 1
    diff_re = partner[0] - current[0]
    diff_im = partner[1] - current[1]
    turned_re, turned_im = twist(diff_re, diff_im, cosine, sine)
    return (
        jnp.where(upper, turned_re, current[0] + partner[0]),
        jnp.where(upper, turned_im, current[1] + partner[1]),
    )


def inverse_section(current, partner, device, level, rows_dev):
    cosine, sine = section_twiddle(device, level, rows_dev, 1.0)
    upper = device >> level & 1 == 1
    moved_re = jnp.where(upper, current[0], partner[0])
    moved_im = jnp.where(upper, current[1], partner[1])
    base_re = jnp.where(upper, partner[0], current[0])
    base_im = jnp.where(upper, partner[1], current[1])
    turned_re, turned_im = twist(moved_re, moved_im, cosine, sine)
    factor = jnp.where(upper, -1.0, 1.0)
    return (base_re + factor * turned_re, base_im + factor * turned_im)


def local_dft(real_part, imag_part, rows_dev, sign):
    index = jnp.arange(rows_dev, dtype=jnp.int32)
    angles = unit_angle(index[:, None] * index[None, :] % rows_dev, rows_dev)
    cosine = jnp.cos(angles)
    sine = sign * jnp.sin(angles)

    def apply_matrix(matrix, data):
        return jnp.einsum("km,emc->ekc", matrix, data, precision=highest)

    new_re = apply_matrix(cosine, real_part) - apply_matrix(sine, imag_part)
    new_im = apply_matrix(cosine, imag_part) + apply_matrix(sine, real_part)
    return (new_re, new_im)


def butterfly_conv(mixed, bank, groups):
    rows_dev, channels = mixed.shape
    devices = lax.axis_size("seq")
    length = rows_dev * devices
    bit_count = devices.bit_length() - 1
    device = lax.axis_index("seq")
    top_level = bit_count - 1
    partner_mixed = swapped(mixed, "seq", top_level)
    current = expand_pair(mixed, device, rows_dev, length)
    partner = expand_pair(partner_mixed, jnp.bitwise_xor(device, 1 << top_level), rows_dev, length)
    state = forward_section(current, partner, device, top_level, rows_dev)
    for level in range(top_level - 1, -1, -1):
        received = swapped(shortened(jnp.stack(state)), "seq", level)
        state = forward_section(state, (received[0], received[1]), device, level, rows_dev)
    spec_re, spec_im = local_dft(state[0], state[1], rows_dev, -1.0)
    residue = jnp.zeros((), jnp.int32)
    for level in range(bit_count):
        residue = residue + ((device >> level & 1) << bit_count - 1 - level)
    freq_even = 2 * (residue + devices * jnp.arange(rows_dev, dtype=jnp.int32))
    freqs = jnp.concatenate([freq_even, freq_even + 1])
    lags = jnp.arange(length, dtype=jnp.int32)
    angles = unit_angle(lags[:, None] * freqs[None, :] % (2 * length), 2 * length)
    table_re = jnp.dot(bank, jnp.cos(angles), precision=highest)
    table_im = -jnp.dot(bank, jnp.sin(angles), precision=highest)
    chosen_re = jnp.take(table_re, groups, axis=0).T.reshape(2, rows_dev, channels)
    chosen_im = jnp.take(table_im, groups, axis=0).T.reshape(2, rows_dev, channels)
    prod_re, prod_im = twist(spec_re, spec_im, chosen_re, chosen_im)
    state = local_dft(prod_re, prod_im, rows_dev, 1.0)
    for level in range(bit_count):
        received = swapped(shortened(jnp.stack(state)), "seq", level)
        state = inverse_section(state, (received[0], received[1]), device, level, rows_dev)
    positions = device * rows_dev + jnp.arange(rows_dev, dtype=jnp.int32)
    final_angles = math.pi / length * positions.astype(jnp.float32)
    cosine = jnp.cos(final_angles)[:, None]
    sine = jnp.sin(final_angles)[:, None]
    return (state[0][0] + cosine * state[0][1] - sine * state[1][1]) / (2.0 * length)


def attention(att_queries, att_keys, hyena_out, block_mask):
    rows_dev, channels = att_queries.shape
    head_count = channels // HD
    device = lax.axis_index("seq")
    block_count = block_mask.shape[1]
    queries = att_queries.reshape(rows_dev, head_count, HD)
    mask_rows = jnp.repeat(block_mask, ABLK, axis=0).astype(jnp.float32)
    query_pos = device * rows_dev + jnp.arange(rows_dev, dtype=jnp.int32)
    scale = HD ** (-0.5)
    key_piece = lax.all_gather(att_keys, "seq", axis=0, tiled=True)
    value_piece = lax.all_gather(hyena_out, "seq", axis=0, tiled=True)
    piece_rows = key_piece.shape[0]
    key_pos = jnp.arange(piece_rows, dtype=jnp.int32)
    onehot = (
        jnp.arange(block_count, dtype=jnp.int32)[:, None] == (key_pos // ABLK)[None, :]
    ).astype(jnp.float32)
    allowed = (jnp.dot(mask_rows, onehot, preferred_element_type=jnp.float32) > 0.5) & (
        key_pos[None, :] <= query_pos[:, None]
    )
    keys_here = key_piece.reshape(piece_rows, head_count, HD)
    values_here = value_piece.reshape(piece_rows, head_count, HD)
    scores = (
        jnp.einsum("thd,shd->hts", queries, keys_here, preferred_element_type=jnp.float32) * scale
    )
    scores = jnp.where(allowed[None], scores, -1e30)
    old_max = jnp.full((head_count, rows_dev), -1e30, jnp.float32)
    new_max = jnp.maximum(old_max, jnp.max(scores, axis=-1))
    weights = jnp.where(allowed[None], jnp.exp(scores - new_max[..., None]), 0.0)
    new_total = jnp.sum(weights, axis=-1)
    new_acc = jnp.einsum(
        "hts,shd->htd",
        weights.astype(jnp.bfloat16),
        values_here,
        preferred_element_type=jnp.float32,
    )
    result = new_acc / new_total[..., None]
    return result.transpose(1, 0, 2).reshape(rows_dev, channels).astype(jnp.bfloat16)


def on_device(
    hyena_query, hyena_key, hyena_value, bias, groups, filters, att_queries, att_keys, block_mask
):
    mixed = (hyena_key.astype(jnp.float32) * hyena_value.astype(jnp.float32)).astype(jnp.bfloat16)
    bank = lax.all_gather(filters.astype(jnp.bfloat16), "chan", axis=0, tiled=True).astype(
        filters.dtype
    )
    bank = lax.all_gather(bank.astype(jnp.bfloat16), "seq", axis=1, tiled=True).astype(bank.dtype)
    conv = butterfly_conv(mixed, bank, groups)
    hyena_out = (
        hyena_query.astype(jnp.float32) * (conv + bias[None, :] * mixed.astype(jnp.float32))
    ).astype(jnp.bfloat16)
    attn_out = attention(att_queries, att_keys, hyena_out, block_mask)
    return (hyena_out, attn_out)


MIXED, SELECT, GATE, QUERY, KEY, HYENA, ATTN, MASK = range(8)


def half_step_dft(block):
    freqs = np.concatenate([np.arange(0, block, 2), np.arange(1, block, 2)])
    steps = (2 * freqs[:, None] + 1) * np.arange(block)[None, :] % (4 * block)
    angles = steps * (math.pi / (2 * block))
    forward = np.concatenate([np.cos(angles), -np.sin(angles)], axis=0)
    inverse = forward.T / block
    return forward.astype(ml_dtypes.bfloat16), inverse.astype(ml_dtypes.bfloat16)


def fused_kernel(
    n, m,
    hk, hv, fil, grp, bias, mask, fwd, inv, hq, aq, ak,
    hy, at,
    mixed, select, bank, masks, mixed_in, select_in, gate_in, query_in, key_in,
    values, result, mask_add, spec, fspec,
    bank_send, bank_recv, send, recv, local,
):
    me = lax.axis_index("seq")
    plane = lax.axis_index("chan")
    rows = hk.shape[0]
    wide = hk.shape[1] // n
    subs = rows // ABLK
    heads = wide // HD
    bf16, f32 = jnp.bfloat16, jnp.float32

    barrier = pltpu.get_barrier_semaphore()
    for d in range(1, n):
        pl.semaphore_signal(
            barrier, inc=1, device_id={"seq": lax.rem(me + d, n)},
            device_id_type=pl.DeviceIdType.MESH,
        )
    for d in range(1, m):
        pl.semaphore_signal(
            barrier, inc=1, device_id={"chan": lax.rem(plane + d, m)},
            device_id_type=pl.DeviceIdType.MESH,
        )

    def columns(p):
        return pl.ds(pl.multiple_of(p * wide, wide), wide)

    def seq_copy(kind, d, src, dst):
        return pltpu.make_async_remote_copy(
            src_ref=src, dst_ref=dst, send_sem=send.at[kind, d], recv_sem=recv.at[kind, d],
            device_id={"seq": lax.rem(me + d, n)}, device_id_type=pl.DeviceIdType.MESH,
        )

    def bank_copy(d):
        return pltpu.make_async_remote_copy(
            src_ref=bank.at[plane], dst_ref=bank.at[plane],
            send_sem=bank_send.at[d], recv_sem=bank_recv.at[d],
            device_id={"chan": lax.rem(plane + d, m)}, device_id_type=pl.DeviceIdType.MESH,
        )

    def mixed_copy(d):
        return seq_copy(MIXED, d, mixed.at[lax.rem(me + d, n)], mixed_in.at[me])

    def select_copy(d):
        return seq_copy(SELECT, d, select.at[lax.rem(me + d, n)], select_in.at[me])

    def gate_copy(d):
        return seq_copy(GATE, d, hq.at[:, columns(lax.rem(me + d, n))], gate_in.at[me])

    def query_copy(d):
        return seq_copy(QUERY, d, aq.at[:, columns(lax.rem(me + d, n))], query_in.at[me])

    def key_copy(d):
        return seq_copy(KEY, d, ak.at[:, columns(lax.rem(me + d, n))], key_in.at[me])

    def hyena_copy(d):
        return seq_copy(HYENA, d, values.at[lax.rem(me + d, n)], hy.at[:, columns(me)])

    def attn_copy(d):
        return seq_copy(ATTN, d, result.at[lax.rem(me + d, n)], at.at[:, columns(me)])

    def mask_copy(d):
        return seq_copy(MASK, d, masks.at[me], masks.at[me])

    own_in = [
        pltpu.make_async_copy(src.at[:, columns(me)], dst.at[me], local.at[i])
        for i, (src, dst) in enumerate([(hq, gate_in), (aq, query_in), (ak, key_in)])
    ]
    for copy in own_in:
        copy.start()

    bank[plane] = fil[...].T.astype(bf16)
    masks[me] = jnp.zeros(masks.shape[1:], f32)
    masks[me, 0:subs, 0:mask.shape[1]] = mask[...].astype(f32)
    for p in range(n):
        part = slice(p * wide, (p + 1) * wide)
        mixed[p] = (hk[:, part].astype(f32) * hv[:, part].astype(f32)).astype(bf16)

    pl.semaphore_wait(barrier, n + m - 2)
    for d in range(1, m):
        bank_copy(d).start()
    for d in range(1, n):
        mixed_copy(d).start()
    for d in range(1, n):
        mask_copy(d).start()

    mixed_in[me] = mixed[me]

    for d in range(1, m):
        bank_copy(d).wait()

    def chosen(p):
        table = jnp.concatenate([bank[k] for k in range(m)], axis=1)
        index = lax.broadcasted_iota(jnp.int32, (table.shape[1], wide), 0)
        onehot = jnp.where(index == grp[p], 1.0, 0.0).astype(bf16)
        return jnp.dot(table, onehot, preferred_element_type=f32).astype(bf16)

    def choose(d, carry):
        p = lax.rem(me + d, n)
        select[p] = chosen(p)
        select_copy(d).start()
        return carry

    lax.fori_loop(1, n, choose, 0)
    select_in[me] = chosen(me)

    spec[me] = jnp.dot(fwd[...], mixed_in[me], preferred_element_type=f32)
    fspec[me] = jnp.dot(fwd[...], select_in[me], preferred_element_type=f32)

    def signal_step(d, carry):
        mixed_copy(d).wait()
        i = lax.rem(me + n - d, n)
        spec[i] = jnp.dot(fwd[...], mixed_in[i], preferred_element_type=f32)
        return carry

    lax.fori_loop(1, n, signal_step, 0)
    for d in range(1, n):
        gate_copy(d).start()

    def filter_step(d, carry):
        select_copy(d).wait()
        i = lax.rem(me + n - d, n)
        fspec[i] = jnp.dot(fwd[...], select_in[i], preferred_element_type=f32)
        return carry

    lax.fori_loop(1, n, filter_step, 0)
    for d in range(1, n):
        query_copy(d).start()
    for d in range(1, n):
        key_copy(d).start()

    tiles = rows // 8

    def product(t, carry):
        re = pl.ds(pl.multiple_of(t * 8, 8), 8)
        im = pl.ds(pl.multiple_of(rows + t * 8, 8), 8)
        turn = jnp.where(t < tiles // 2, 1.0, -1.0).astype(f32)
        for lane in range(0, wide, 128):
            lanes = slice(lane, lane + 128)
            xr = [spec[i, re, lanes] for i in range(n)]
            xi = [spec[i, im, lanes] for i in range(n)]
            gr = [fspec[i, re, lanes] for i in range(n)]
            gi = [fspec[i, im, lanes] for i in range(n)]
            last_re = last_im = None
            for j in range(n):
                sum_re = sum_im = None
                for i in range(j + 1):
                    a, b, c, e = xr[i], xi[i], gr[j - i], gi[j - i]
                    new_re, new_im = a * c - b * e, a * e + b * c
                    sum_re = new_re if sum_re is None else sum_re + new_re
                    sum_im = new_im if sum_im is None else sum_im + new_im
                if j == 0:
                    spec[j, re, lanes] = sum_re
                    spec[j, im, lanes] = sum_im
                else:
                    spec[j, re, lanes] = sum_re - turn * last_im
                    spec[j, im, lanes] = sum_im + turn * last_re
                last_re, last_im = sum_re, sum_im
        return carry

    lax.fori_loop(0, tiles, product, 0)

    own_in[0].wait()

    def finish(j):
        conv = jnp.dot(inv[...], spec[j].astype(bf16), preferred_element_type=f32)
        direct = bias[me] * mixed_in[j].astype(f32)
        values[j] = (gate_in[j].astype(f32) * (conv + direct)).astype(bf16)

    def hyena_step(d, carry):
        gate_copy(n - d).wait()
        finish(lax.rem(me + d, n))
        hyena_copy(d).start()
        return carry

    lax.fori_loop(1, n, hyena_step, 0)
    finish(me)
    own_hyena = pltpu.make_async_copy(values.at[me], hy.at[:, columns(me)], local.at[3])
    own_hyena.start()

    for d in range(1, n):
        mask_copy(d).wait()
    flags = masks[...].reshape(n * masks.shape[1], masks.shape[2]).astype(bf16)
    for k in range(n):
        block_id = lax.broadcasted_iota(jnp.int32, (masks.shape[2], rows), 0)
        owner = lax.broadcasted_iota(jnp.int32, (masks.shape[2], rows), 1) // ABLK + k * subs
        spread = jnp.where(block_id == owner, 1.0, 0.0).astype(bf16)
        shown = jnp.dot(flags, spread, preferred_element_type=f32)
        mask_add[:, k] = ((shown - 1.0) * 1e30).reshape(n, masks.shape[1], rows)

    own_in[1].wait()
    own_in[2].wait()
    for d in range(1, n):
        query_copy(d).wait()
    for d in range(1, n):
        key_copy(d).wait()
    scale = HD ** (-0.5)

    def attend(r):

        def scores(h, k, add):
            part = slice(h * HD, (h + 1) * HD)
            raw = lax.dot_general(
                query_in[r, :, part], key_in[k, :, part], (((1,), (1,)), ((), ())),
                preferred_element_type=f32,
            )
            return raw + add

        def weighted(h, k, weights):
            part = slice(h * HD, (h + 1) * HD)
            return jnp.dot(weights.astype(bf16), values[k, :, part], preferred_element_type=f32)

        def added(k):
            flags_here = mask_add[r, k]
            return jnp.concatenate(
                [jnp.broadcast_to(flags_here[i : i + 1], (ABLK, rows)) for i in range(subs)], axis=0
            )

        row = lax.broadcasted_iota(jnp.int32, (rows, rows), 0)
        col = lax.broadcasted_iota(jnp.int32, (rows, rows), 1)
        add = jnp.where(col <= row, added(r), -1e30)
        state = []
        for h in range(heads):
            here = scores(h, r, add)
            top = jnp.max(here, axis=1, keepdims=True)
            weights = jnp.exp((here - top) * scale)
            state.append((top, jnp.sum(weights, axis=1, keepdims=True), weighted(h, r, weights)))

        def step(k, state):
            add = added(k)
            out = []
            for h in range(heads):
                top, total, acc = state[h]
                here = scores(h, k, add)
                new_top = jnp.maximum(top, jnp.max(here, axis=1, keepdims=True))
                weights = jnp.exp((here - new_top) * scale)
                keep = jnp.exp((top - new_top) * scale)
                total = total * keep + jnp.sum(weights, axis=1, keepdims=True)
                out.append((new_top, total, acc * keep + weighted(h, k, weights)))
            return tuple(out)

        state = lax.fori_loop(0, r, step, tuple(state))
        for h in range(heads):
            result[r, :, h * HD : (h + 1) * HD] = (state[h][2] / state[h][1]).astype(bf16)

    def attn_step(d, carry):
        attend(lax.rem(me + d, n))
        attn_copy(d).start()
        return carry

    lax.fori_loop(1, n, attn_step, 0)
    attend(me)
    own_attn = pltpu.make_async_copy(result.at[me], at.at[:, columns(me)], local.at[4])
    own_attn.start()
    own_hyena.wait()
    own_attn.wait()
    for d in range(1, n):
        hyena_copy(d).wait()
    for d in range(1, n):
        attn_copy(d).wait()


def fused_on_device(
    n, m, hyena_query, hyena_key, hyena_value, bias, groups, filters, att_queries, att_keys, block_mask
):
    rows, channels = hyena_key.shape
    wide = channels // n
    lanes = filters.shape[0]
    forward, inverse = half_step_dft(rows)
    bf16, f32 = jnp.bfloat16, jnp.float32
    blocks = pltpu.VMEM((n, rows, wide), bf16)
    vmem = pl.BlockSpec(memory_space=pltpu.VMEM)
    anywhere = pl.BlockSpec(memory_space=pl.ANY)
    return pl.pallas_call(
        functools.partial(fused_kernel, n, m),
        out_shape=[jax.ShapeDtypeStruct((rows, channels), bf16)] * 2,
        in_specs=[vmem] * 8 + [anywhere] * 3,
        out_specs=[anywhere] * 2,
        scratch_shapes=[
            blocks,
            blocks,
            pltpu.VMEM((m, rows, lanes), bf16),
            pltpu.VMEM((n, 8, 128), f32),
            blocks,
            blocks,
            blocks,
            blocks,
            blocks,
            blocks,
            blocks,
            pltpu.VMEM((n, n, 8, rows), f32),
            pltpu.VMEM((n, 2 * rows, wide), f32),
            pltpu.VMEM((n, 2 * rows, wide), f32),
            pltpu.SemaphoreType.DMA((m,)),
            pltpu.SemaphoreType.DMA((m,)),
            pltpu.SemaphoreType.DMA((8, n)),
            pltpu.SemaphoreType.DMA((8, n)),
            pltpu.SemaphoreType.DMA((5,)),
        ],
        compiler_params=pltpu.CompilerParams(
            collective_id=0, has_side_effects=True, vmem_limit_bytes=52 * 1024 * 1024
        ),
        name="hyena_attention",
    )(
        hyena_key, hyena_value, filters,
        groups.reshape(n, 1, wide), bias.reshape(n, 1, wide), block_mask,
        jnp.asarray(forward), jnp.asarray(inverse),
        hyena_query, att_queries, att_keys,
    )


def by_shape(
    n, m, hyena_query, hyena_key, hyena_value, bias, groups, filters, att_queries, att_keys, block_mask
):
    rows, channels = hyena_key.shape
    fits = (
        channels % (n * HD) == 0
        and rows % (2 * ABLK) == 0
        and rows // ABLK <= 8
        and block_mask.shape[1] <= 128
        and filters.shape[0] % 128 == 0
        and filters.shape[1] == rows
    )
    args = (
        hyena_query, hyena_key, hyena_value, bias, groups, filters, att_queries, att_keys, block_mask
    )
    return fused_on_device(n, m, *args) if fits else on_device(*args)


def solution(mesh):
    return jax.shard_map(
        functools.partial(by_shape, mesh.shape["seq"], mesh.shape["chan"]),
        mesh=mesh,
        in_specs=(
            P("seq", "chan"),
            P("seq", "chan"),
            P("seq", "chan"),
            P("chan"),
            P("chan"),
            P("chan", "seq"),
            P("seq", "chan"),
            P("seq", "chan"),
            P("seq", None),
        ),
        out_specs=(P("seq", "chan"), P("seq", "chan")),
        check_vma=False,
    )
```

```python
import functools
import math

import jax
import jax.numpy as jnp
import ml_dtypes
import numpy as np
from jax import lax
from jax.experimental import pallas as pl
from jax.experimental.pallas import tpu as pltpu
from jax.sharding import PartitionSpec as P

HD = 128
ABLK = 128


highest = lax.Precision.HIGHEST


def swapped(value, axis, stride):
    mask = 2**stride
    pairs = [(source, source ^ mask) for source in range(lax.axis_size(axis))]
    return lax.ppermute(value, axis, pairs)


def shortened(x):

    def short(part):
        return part.astype(jnp.bfloat16) if part.dtype == jnp.float32 else part

    return jax.tree.map(short, x)


def unit_angle(numer, denom):
    return 2.0 * math.pi / denom * numer.astype(jnp.float32)


def twist(real_part, imag_part, cosine, sine):
    return (real_part * cosine - imag_part * sine, real_part * sine + imag_part * cosine)


def expand_pair(signal, device, rows_dev, length):
    positions = device * rows_dev + jnp.arange(rows_dev, dtype=jnp.int32)
    angles = math.pi / length * positions.astype(jnp.float32)
    values = signal.astype(jnp.float32)
    cosine = jnp.cos(angles)[:, None]
    sine = jnp.sin(angles)[:, None]
    real_part = jnp.stack([values, values * cosine])
    imag_part = jnp.stack([jnp.zeros_like(values), -values * sine])
    return (real_part, imag_part)


def section_twiddle(device, level, rows_dev, sign):
    inner = device % (1 << level) * rows_dev + jnp.arange(rows_dev, dtype=jnp.int32)
    angles = unit_angle(inner, rows_dev << level + 1)
    return (jnp.cos(angles)[:, None], sign * jnp.sin(angles)[:, None])


def forward_section(current, partner, device, level, rows_dev):
    cosine, sine = section_twiddle(device, level, rows_dev, -1.0)
    upper = device >> level & 1 == 1
    diff_re = partner[0] - current[0]
    diff_im = partner[1] - current[1]
    turned_re, turned_im = twist(diff_re, diff_im, cosine, sine)
    return (
        jnp.where(upper, turned_re, current[0] + partner[0]),
        jnp.where(upper, turned_im, current[1] + partner[1]),
    )


def inverse_section(current, partner, device, level, rows_dev):
    cosine, sine = section_twiddle(device, level, rows_dev, 1.0)
    upper = device >> level & 1 == 1
    moved_re = jnp.where(upper, current[0], partner[0])
    moved_im = jnp.where(upper, current[1], partner[1])
    base_re = jnp.where(upper, partner[0], current[0])
    base_im = jnp.where(upper, partner[1], current[1])
    turned_re, turned_im = twist(moved_re, moved_im, cosine, sine)
    factor = jnp.where(upper, -1.0, 1.0)
    return (base_re + factor * turned_re, base_im + factor * turned_im)


def local_dft(real_part, imag_part, rows_dev, sign):
    index = jnp.arange(rows_dev, dtype=jnp.int32)
    angles = unit_angle(index[:, None] * index[None, :] % rows_dev, rows_dev)
    cosine = jnp.cos(angles)
    sine = sign * jnp.sin(angles)

    def apply_matrix(matrix, data):
        return jnp.einsum("km,emc->ekc", matrix, data, precision=highest)

    new_re = apply_matrix(cosine, real_part) - apply_matrix(sine, imag_part)
    new_im = apply_matrix(cosine, imag_part) + apply_matrix(sine, real_part)
    return (new_re, new_im)


def butterfly_conv(mixed, bank, groups):
    rows_dev, channels = mixed.shape
    devices = lax.axis_size("seq")
    length = rows_dev * devices
    bit_count = devices.bit_length() - 1
    device = lax.axis_index("seq")
    top_level = bit_count - 1
    partner_mixed = swapped(mixed, "seq", top_level)
    current = expand_pair(mixed, device, rows_dev, length)
    partner = expand_pair(partner_mixed, jnp.bitwise_xor(device, 1 << top_level), rows_dev, length)
    state = forward_section(current, partner, device, top_level, rows_dev)
    for level in range(top_level - 1, -1, -1):
        received = swapped(shortened(jnp.stack(state)), "seq", level)
        state = forward_section(state, (received[0], received[1]), device, level, rows_dev)
    spec_re, spec_im = local_dft(state[0], state[1], rows_dev, -1.0)
    residue = jnp.zeros((), jnp.int32)
    for level in range(bit_count):
        residue = residue + ((device >> level & 1) << bit_count - 1 - level)
    freq_even = 2 * (residue + devices * jnp.arange(rows_dev, dtype=jnp.int32))
    freqs = jnp.concatenate([freq_even, freq_even + 1])
    lags = jnp.arange(length, dtype=jnp.int32)
    angles = unit_angle(lags[:, None] * freqs[None, :] % (2 * length), 2 * length)
    table_re = jnp.dot(bank, jnp.cos(angles), precision=highest)
    table_im = -jnp.dot(bank, jnp.sin(angles), precision=highest)
    chosen_re = jnp.take(table_re, groups, axis=0).T.reshape(2, rows_dev, channels)
    chosen_im = jnp.take(table_im, groups, axis=0).T.reshape(2, rows_dev, channels)
    prod_re, prod_im = twist(spec_re, spec_im, chosen_re, chosen_im)
    state = local_dft(prod_re, prod_im, rows_dev, 1.0)
    for level in range(bit_count):
        received = swapped(shortened(jnp.stack(state)), "seq", level)
        state = inverse_section(state, (received[0], received[1]), device, level, rows_dev)
    positions = device * rows_dev + jnp.arange(rows_dev, dtype=jnp.int32)
    final_angles = math.pi / length * positions.astype(jnp.float32)
    cosine = jnp.cos(final_angles)[:, None]
    sine = jnp.sin(final_angles)[:, None]
    return (state[0][0] + cosine * state[0][1] - sine * state[1][1]) / (2.0 * length)


def attention(att_queries, att_keys, hyena_out, block_mask):
    rows_dev, channels = att_queries.shape
    head_count = channels // HD
    device = lax.axis_index("seq")
    block_count = block_mask.shape[1]
    queries = att_queries.reshape(rows_dev, head_count, HD)
    mask_rows = jnp.repeat(block_mask, ABLK, axis=0).astype(jnp.float32)
    query_pos = device * rows_dev + jnp.arange(rows_dev, dtype=jnp.int32)
    scale = HD ** (-0.5)
    key_piece = lax.all_gather(att_keys, "seq", axis=0, tiled=True)
    value_piece = lax.all_gather(hyena_out, "seq", axis=0, tiled=True)
    piece_rows = key_piece.shape[0]
    key_pos = jnp.arange(piece_rows, dtype=jnp.int32)
    onehot = (
        jnp.arange(block_count, dtype=jnp.int32)[:, None] == (key_pos // ABLK)[None, :]
    ).astype(jnp.float32)
    allowed = (jnp.dot(mask_rows, onehot, preferred_element_type=jnp.float32) > 0.5) & (
        key_pos[None, :] <= query_pos[:, None]
    )
    keys_here = key_piece.reshape(piece_rows, head_count, HD)
    values_here = value_piece.reshape(piece_rows, head_count, HD)
    scores = (
        jnp.einsum("thd,shd->hts", queries, keys_here, preferred_element_type=jnp.float32) * scale
    )
    scores = jnp.where(allowed[None], scores, -1e30)
    old_max = jnp.full((head_count, rows_dev), -1e30, jnp.float32)
    new_max = jnp.maximum(old_max, jnp.max(scores, axis=-1))
    weights = jnp.where(allowed[None], jnp.exp(scores - new_max[..., None]), 0.0)
    new_total = jnp.sum(weights, axis=-1)
    new_acc = jnp.einsum(
        "hts,shd->htd",
        weights.astype(jnp.bfloat16),
        values_here,
        preferred_element_type=jnp.float32,
    )
    result = new_acc / new_total[..., None]
    return result.transpose(1, 0, 2).reshape(rows_dev, channels).astype(jnp.bfloat16)


def on_device(
    hyena_query, hyena_key, hyena_value, bias, groups, filters, att_queries, att_keys, block_mask
):
    mixed = (hyena_key.astype(jnp.float32) * hyena_value.astype(jnp.float32)).astype(jnp.bfloat16)
    bank = lax.all_gather(filters.astype(jnp.bfloat16), "chan", axis=0, tiled=True).astype(
        filters.dtype
    )
    bank = lax.all_gather(bank.astype(jnp.bfloat16), "seq", axis=1, tiled=True).astype(bank.dtype)
    conv = butterfly_conv(mixed, bank, groups)
    hyena_out = (
        hyena_query.astype(jnp.float32) * (conv + bias[None, :] * mixed.astype(jnp.float32))
    ).astype(jnp.bfloat16)
    attn_out = attention(att_queries, att_keys, hyena_out, block_mask)
    return (hyena_out, attn_out)


MIXED, GATE, QUERY, KEY, HYENA, ATTN, MASK = range(7)


def half_step_dft(block):
    freqs = np.concatenate([np.arange(0, block, 2), np.arange(1, block, 2)])
    steps = (2 * freqs[:, None] + 1) * np.arange(block)[None, :] % (4 * block)
    angles = steps * (math.pi / (2 * block))
    forward = np.concatenate([np.cos(angles), -np.sin(angles)], axis=0)
    inverse = forward.T / block
    return forward.astype(ml_dtypes.bfloat16), inverse.astype(ml_dtypes.bfloat16)


def fused_kernel(
    n, m,
    hk_far, hv_far, fil_far, grp_far, bias_far, mask_far, fwd_far, inv_far, hq, aq, ak,
    hy, at,
    hk, hv, fil, grp, bias, mask, fwd, inv,
    mixed, select, bank, hot, masks, mixed_in, select_in, gate_in, query_in, key_in,
    values, result, mask_add, spec, fspec,
    lag_send, lag_recv, bank_send, bank_recv, pair_send, pair_recv, send, recv, local, loads,
):
    me = lax.axis_index("seq")
    plane = lax.axis_index("chan")
    side = lax.rem(me, 2)
    sibling = me + 1 - 2 * side
    pair = lax.div(me, 2)
    pairs = n // 2
    rows = hk.shape[0]
    wide = hk.shape[1] // n
    subs = rows // ABLK
    heads = wide // HD
    bf16, f32 = jnp.bfloat16, jnp.float32

    barrier = pltpu.get_barrier_semaphore()
    for d in range(1, n):
        pl.semaphore_signal(
            barrier, inc=1, device_id={"seq": lax.rem(me + d, n)},
            device_id_type=pl.DeviceIdType.MESH,
        )
    for d in range(1, m):
        pl.semaphore_signal(
            barrier, inc=1, device_id={"chan": lax.rem(plane + d, m)},
            device_id_type=pl.DeviceIdType.MESH,
        )

    def columns(p):
        return pl.ds(pl.multiple_of(p * wide, wide), wide)

    def seq_copy(kind, d, src, dst):
        return pltpu.make_async_remote_copy(
            src_ref=src, dst_ref=dst, send_sem=send.at[kind, d], recv_sem=recv.at[kind, d],
            device_id={"seq": lax.rem(me + d, n)}, device_id_type=pl.DeviceIdType.MESH,
        )

    def lag_copy(e):
        return pltpu.make_async_remote_copy(
            src_ref=bank.at[plane, pair], dst_ref=bank.at[plane, pair],
            send_sem=lag_send.at[e], recv_sem=lag_recv.at[e],
            device_id={"seq": lax.rem(me + 2 * e, n)}, device_id_type=pl.DeviceIdType.MESH,
        )

    def bank_copy(e, d):
        part = lax.rem(pair + pairs - e, pairs)
        return pltpu.make_async_remote_copy(
            src_ref=bank.at[plane, part], dst_ref=bank.at[plane, part],
            send_sem=bank_send.at[e, d], recv_sem=bank_recv.at[e, d],
            device_id={"chan": lax.rem(plane + d, m)}, device_id_type=pl.DeviceIdType.MESH,
        )

    def pair_copy(e):
        part = 2 * lax.rem(pair + pairs - e, pairs) + side
        return pltpu.make_async_remote_copy(
            src_ref=select.at[e], dst_ref=select_in.at[part],
            send_sem=pair_send.at[e], recv_sem=pair_recv.at[e],
            device_id={"seq": sibling}, device_id_type=pl.DeviceIdType.MESH,
        )

    def mixed_copy(d):
        return seq_copy(MIXED, d, mixed.at[lax.rem(me + d, n)], mixed_in.at[me])

    def gate_copy(d):
        return seq_copy(GATE, d, hq.at[:, columns(lax.rem(me + d, n))], gate_in.at[me])

    def query_copy(d):
        return seq_copy(QUERY, d, aq.at[:, columns(lax.rem(me + d, n))], query_in.at[me])

    def key_copy(d):
        return seq_copy(KEY, d, ak.at[:, columns(lax.rem(me + d, n))], key_in.at[me])

    def hyena_copy(d):
        return seq_copy(HYENA, d, values.at[lax.rem(me + d, n)], hy.at[:, columns(me)])

    def attn_copy(d):
        return seq_copy(ATTN, d, result.at[lax.rem(me + d, n)], at.at[:, columns(me)])

    def mask_copy(d):
        return seq_copy(MASK, d, masks.at[me], masks.at[me])

    own_in = [
        pltpu.make_async_copy(src.at[:, columns(me)], dst.at[me], local.at[i])
        for i, (src, dst) in enumerate([(hq, gate_in), (aq, query_in), (ak, key_in)])
    ]
    for copy in own_in:
        copy.start()

    near = [
        pltpu.make_async_copy(src, dst, loads.at[i])
        for i, (src, dst) in enumerate([
            (fil_far, fil), (mask_far, mask), (hk_far, hk), (hv_far, hv),
            (grp_far, grp), (fwd_far, fwd), (inv_far, inv), (bias_far, bias),
        ])
    ]
    for copy in near:
        copy.start()

    near[0].wait()
    near[1].wait()
    bank[plane, pair] = fil[...].T.astype(bf16)
    masks[me] = jnp.zeros(masks.shape[1:], f32)
    masks[me, 0:subs, 0 : mask.shape[1]] = mask[...].astype(f32)
    near[2].wait()
    near[3].wait()
    for p in range(n):
        part = slice(p * wide, (p + 1) * wide)
        mixed[p] = (hk[:, part].astype(f32) * hv[:, part].astype(f32)).astype(bf16)

    pl.semaphore_wait(barrier, n + m - 2)
    for e in range(1, pairs):
        lag_copy(e).start()
    for d in range(1, m):
        bank_copy(0, d).start()
    for d in range(1, n):
        mixed_copy(d).start()
    for d in range(1, n):
        mask_copy(d).start()

    mixed_in[me] = mixed[me]
    near[4].wait()
    lanes_here = bank.shape[3]
    for which, owner in enumerate((me, sibling)):
        index = lax.broadcasted_iota(jnp.int32, (m * lanes_here, wide), 0)
        hot[which] = jnp.where(index == grp[owner], 1.0, 0.0).astype(bf16)

    for e in range(1, pairs):
        lag_copy(e).wait()
        for d in range(1, m):
            bank_copy(e, d).start()

    near[5].wait()
    spec[me] = jnp.dot(fwd[...], mixed_in[me], preferred_element_type=f32)

    def signal_step(d, carry):
        mixed_copy(d).wait()
        i = lax.rem(me + n - d, n)
        spec[i] = jnp.dot(fwd[...], mixed_in[i], preferred_element_type=f32)
        return carry

    lax.fori_loop(1, n // 2 + 1, signal_step, 0)
    for d in range(1, n):
        gate_copy(d).start()
    lax.fori_loop(n // 2 + 1, n, signal_step, 0)

    def chosen(part, which):
        table = jnp.concatenate([bank[k, part] for k in range(m)], axis=1)
        return jnp.dot(table, hot[which], preferred_element_type=f32).astype(bf16)

    for e in range(pairs):
        for d in range(1, m):
            bank_copy(e, d).wait()
        part = lax.rem(pair + pairs - e, pairs)
        select[e] = chosen(part, 1)
        pair_copy(e).start()
        own = 2 * part + side
        fspec[own] = jnp.dot(fwd[...], chosen(part, 0), preferred_element_type=f32)
        if e == 0:
            for d in range(1, n):
                query_copy(d).start()
        if e == min(1, pairs - 1):
            for d in range(1, n):
                key_copy(d).start()
    for e in range(pairs):
        pair_copy(e).wait()
        other = 2 * lax.rem(pair + pairs - e, pairs) + 1 - side
        fspec[other] = jnp.dot(fwd[...], select_in[other], preferred_element_type=f32)

    tiles = rows // 8

    def product(t, carry):
        re = pl.ds(pl.multiple_of(t * 8, 8), 8)
        im = pl.ds(pl.multiple_of(rows + t * 8, 8), 8)
        turn = jnp.where(t < tiles // 2, 1.0, -1.0).astype(f32)
        for lane in range(0, wide, 128):
            lanes = slice(lane, lane + 128)
            xr = [spec[i, re, lanes] for i in range(n)]
            xi = [spec[i, im, lanes] for i in range(n)]
            gr = [fspec[i, re, lanes] for i in range(n)]
            gi = [fspec[i, im, lanes] for i in range(n)]
            last_re = last_im = None
            for j in range(n):
                sum_re = sum_im = None
                for i in range(j + 1):
                    a, b, c, e = xr[i], xi[i], gr[j - i], gi[j - i]
                    new_re, new_im = a * c - b * e, a * e + b * c
                    sum_re = new_re if sum_re is None else sum_re + new_re
                    sum_im = new_im if sum_im is None else sum_im + new_im
                if j == 0:
                    spec[j, re, lanes] = sum_re
                    spec[j, im, lanes] = sum_im
                else:
                    spec[j, re, lanes] = sum_re - turn * last_im
                    spec[j, im, lanes] = sum_im + turn * last_re
                last_re, last_im = sum_re, sum_im
        return carry

    lax.fori_loop(0, tiles, product, 0)

    own_in[0].wait()
    near[6].wait()
    near[7].wait()

    def finish(j):
        conv = jnp.dot(inv[...], spec[j].astype(bf16), preferred_element_type=f32)
        direct = bias[me] * mixed_in[j].astype(f32)
        values[j] = (gate_in[j].astype(f32) * (conv + direct)).astype(bf16)

    def hyena_step(d, carry):
        gate_copy(n - d).wait()
        finish(lax.rem(me + d, n))
        return carry

    lax.fori_loop(1, n, hyena_step, 0)
    finish(me)
    own_hyena = pltpu.make_async_copy(values.at[me], hy.at[:, columns(me)], local.at[3])
    own_hyena.start()

    for d in range(1, n):
        mask_copy(d).wait()
    flags = masks[...].reshape(n * masks.shape[1], masks.shape[2]).astype(bf16)
    for k in range(n):
        block_id = lax.broadcasted_iota(jnp.int32, (masks.shape[2], rows), 0)
        owner = lax.broadcasted_iota(jnp.int32, (masks.shape[2], rows), 1) // ABLK + k * subs
        spread = jnp.where(block_id == owner, 1.0, 0.0).astype(bf16)
        shown = jnp.dot(flags, spread, preferred_element_type=f32)
        mask_add[:, k] = ((shown - 1.0) * 1e30).reshape(n, masks.shape[1], rows)

    own_in[1].wait()
    own_in[2].wait()
    for d in range(1, n):
        query_copy(d).wait()
    for d in range(1, n // 2 + 1):
        key_copy(d).wait()
    for d in range(1, n):
        hyena_copy(d).start()
    for d in range(n // 2 + 1, n):
        key_copy(d).wait()
    scale = HD ** (-0.5) / math.log(2.0)

    def lane_sum(weights):
        total = weights[:, 0:128]
        for lane in range(128, rows, 128):
            total = total + weights[:, lane : lane + 128]
        return total

    def attend(r):

        def scores(h, k, add):
            part = slice(h * HD, (h + 1) * HD)
            raw = lax.dot_general(
                query_in[r, :, part], key_in[k, :, part], (((1,), (1,)), ((), ())),
                preferred_element_type=f32,
            )
            return raw + add

        def weighted(h, k, weights):
            part = slice(h * HD, (h + 1) * HD)
            return jnp.dot(weights.astype(bf16), values[k, :, part], preferred_element_type=f32)

        def added(k):
            flags_here = mask_add[r, k]
            return jnp.concatenate(
                [jnp.broadcast_to(flags_here[i : i + 1], (ABLK, rows)) for i in range(subs)], axis=0
            )

        row = lax.broadcasted_iota(jnp.int32, (rows, rows), 0)
        col = lax.broadcasted_iota(jnp.int32, (rows, rows), 1)
        add = jnp.where(col <= row, added(r), -1e30)
        state = []
        for h in range(heads):
            here = scores(h, r, add)
            top = jnp.max(here, axis=1, keepdims=True)
            weights = jnp.exp2((here - top) * scale)
            state.append((top, lane_sum(weights), weighted(h, r, weights)))

        def step(k, state):
            add = added(k)
            out = []
            for h in range(heads):
                top, total, acc = state[h]
                here = scores(h, k, add)
                new_top = jnp.maximum(top, jnp.max(here, axis=1, keepdims=True))
                weights = jnp.exp2((here - new_top) * scale)
                keep = jnp.exp2((top - new_top) * scale)
                total = total * keep + lane_sum(weights)
                out.append((new_top, total, acc * keep + weighted(h, k, weights)))
            return tuple(out)

        state = lax.fori_loop(0, r, step, tuple(state))
        for h in range(heads):
            total = jnp.sum(state[h][1], axis=1, keepdims=True)
            result[r, :, h * HD : (h + 1) * HD] = (state[h][2] / total).astype(bf16)

    def attn_step(d, carry):
        attend(lax.rem(me + d, n))
        attn_copy(d).start()
        return carry

    lax.fori_loop(1, n, attn_step, 0)
    attend(me)
    own_attn = pltpu.make_async_copy(result.at[me], at.at[:, columns(me)], local.at[4])
    own_attn.start()
    own_hyena.wait()
    own_attn.wait()
    for d in range(1, n):
        hyena_copy(d).wait()
    for d in range(1, n):
        attn_copy(d).wait()


def copy_kernel(parts, hy, at, hy_out, at_out, sems):
    step = hy.shape[0] // parts
    copies = []
    for i, (src, dst) in enumerate([(hy, hy_out), (at, at_out)]):
        for k in range(parts):
            part = pl.ds(k * step, step)
            copies.append(pltpu.make_async_copy(src.at[part], dst.at[part], sems.at[i, k]))
    for copy in copies:
        copy.start()
    for copy in copies:
        copy.wait()


def fused_on_device(
    n, m, hyena_query, hyena_key, hyena_value, bias, groups, filters, att_queries, att_keys, block_mask
):
    rows, channels = hyena_key.shape
    wide = channels // n
    lanes = filters.shape[0]
    pairs = n // 2
    forward, inverse = half_step_dft(rows)
    bf16, f32 = jnp.bfloat16, jnp.float32
    blocks = pltpu.VMEM((n, rows, wide), bf16)
    anywhere = pl.BlockSpec(memory_space=pl.ANY)
    dma = pltpu.SemaphoreType.DMA
    outs = [jax.ShapeDtypeStruct((rows, channels), bf16)] * 2
    hyena_out, attn_out = pl.pallas_call(
        functools.partial(fused_kernel, n, m),
        out_shape=outs,
        in_specs=[anywhere] * 11,
        out_specs=[anywhere] * 2,
        scratch_shapes=[
            pltpu.VMEM((rows, channels), bf16),
            pltpu.VMEM((rows, channels), bf16),
            pltpu.VMEM(filters.shape, f32),
            pltpu.VMEM((n, 1, wide), jnp.int32),
            pltpu.VMEM((n, 1, wide), f32),
            pltpu.VMEM(block_mask.shape, jnp.int32),
            pltpu.VMEM(forward.shape, bf16),
            pltpu.VMEM(inverse.shape, bf16),
            blocks,
            pltpu.VMEM((pairs, rows, wide), bf16),
            pltpu.VMEM((m, pairs, rows, lanes), bf16),
            pltpu.VMEM((2, m * lanes, wide), bf16),
            pltpu.VMEM((n, 8, 128), f32),
            blocks,
            blocks,
            blocks,
            blocks,
            blocks,
            blocks,
            blocks,
            pltpu.VMEM((n, n, 8, rows), f32),
            pltpu.VMEM((n, 2 * rows, wide), f32),
            pltpu.VMEM((n, 2 * rows, wide), f32),
            dma((pairs,)),
            dma((pairs,)),
            dma((pairs, m)),
            dma((pairs, m)),
            dma((pairs,)),
            dma((pairs,)),
            dma((7, n)),
            dma((7, n)),
            dma((5,)),
            dma((8,)),
        ],
        compiler_params=pltpu.CompilerParams(
            collective_id=0, has_side_effects=True, vmem_limit_bytes=60 * 1024 * 1024
        ),
        name="hyena_attention",
    )(
        hyena_key, hyena_value, filters,
        groups.reshape(n, 1, wide), bias.reshape(n, 1, wide), block_mask,
        jnp.asarray(forward), jnp.asarray(inverse),
        hyena_query, att_queries, att_keys,
    )
    parts = 2
    return pl.pallas_call(
        functools.partial(copy_kernel, parts),
        out_shape=outs,
        in_specs=[anywhere] * 2,
        out_specs=[anywhere] * 2,
        scratch_shapes=[dma((2, parts))],
        compiler_params=pltpu.CompilerParams(vmem_limit_bytes=60 * 1024 * 1024),
        name="results",
    )(hyena_out, attn_out)


def by_shape(
    n, m, hyena_query, hyena_key, hyena_value, bias, groups, filters, att_queries, att_keys, block_mask
):
    rows, channels = hyena_key.shape
    fits = (
        channels % (n * HD) == 0
        and n % 2 == 0
        and rows % (2 * ABLK) == 0
        and rows // ABLK <= 8
        and block_mask.shape[1] <= 128
        and filters.shape[0] % 128 == 0
        and filters.shape[1] == rows
    )
    args = (
        hyena_query, hyena_key, hyena_value, bias, groups, filters, att_queries, att_keys, block_mask
    )
    return fused_on_device(n, m, *args) if fits else on_device(*args)


def solution(mesh):
    return jax.shard_map(
        functools.partial(by_shape, mesh.shape["seq"], mesh.shape["chan"]),
        mesh=mesh,
        in_specs=(
            P("seq", "chan"),
            P("seq", "chan"),
            P("seq", "chan"),
            P("chan"),
            P("chan"),
            P("chan", "seq"),
            P("seq", "chan"),
            P("seq", "chan"),
            P("seq", None),
        ),
        out_specs=(P("seq", "chan"), P("seq", "chan")),
        check_vma=False,
    )
```

```python
import functools
import math

import jax
import jax.numpy as jnp
import ml_dtypes
import numpy as np
from jax import lax
from jax.experimental import pallas as pl
from jax.experimental.pallas import tpu as pltpu
from jax.sharding import PartitionSpec as P

HD = 128
ABLK = 128


highest = lax.Precision.HIGHEST


def swapped(value, axis, stride):
    mask = 2**stride
    pairs = [(source, source ^ mask) for source in range(lax.axis_size(axis))]
    return lax.ppermute(value, axis, pairs)


def shortened(x):

    def short(part):
        return part.astype(jnp.bfloat16) if part.dtype == jnp.float32 else part

    return jax.tree.map(short, x)


def unit_angle(numer, denom):
    return 2.0 * math.pi / denom * numer.astype(jnp.float32)


def twist(real_part, imag_part, cosine, sine):
    return (real_part * cosine - imag_part * sine, real_part * sine + imag_part * cosine)


def expand_pair(signal, device, rows_dev, length):
    positions = device * rows_dev + jnp.arange(rows_dev, dtype=jnp.int32)
    angles = math.pi / length * positions.astype(jnp.float32)
    values = signal.astype(jnp.float32)
    cosine = jnp.cos(angles)[:, None]
    sine = jnp.sin(angles)[:, None]
    real_part = jnp.stack([values, values * cosine])
    imag_part = jnp.stack([jnp.zeros_like(values), -values * sine])
    return (real_part, imag_part)


def section_twiddle(device, level, rows_dev, sign):
    inner = device % (1 << level) * rows_dev + jnp.arange(rows_dev, dtype=jnp.int32)
    angles = unit_angle(inner, rows_dev << level + 1)
    return (jnp.cos(angles)[:, None], sign * jnp.sin(angles)[:, None])


def forward_section(current, partner, device, level, rows_dev):
    cosine, sine = section_twiddle(device, level, rows_dev, -1.0)
    upper = device >> level & 1 == 1
    diff_re = partner[0] - current[0]
    diff_im = partner[1] - current[1]
    turned_re, turned_im = twist(diff_re, diff_im, cosine, sine)
    return (
        jnp.where(upper, turned_re, current[0] + partner[0]),
        jnp.where(upper, turned_im, current[1] + partner[1]),
    )


def inverse_section(current, partner, device, level, rows_dev):
    cosine, sine = section_twiddle(device, level, rows_dev, 1.0)
    upper = device >> level & 1 == 1
    moved_re = jnp.where(upper, current[0], partner[0])
    moved_im = jnp.where(upper, current[1], partner[1])
    base_re = jnp.where(upper, partner[0], current[0])
    base_im = jnp.where(upper, partner[1], current[1])
    turned_re, turned_im = twist(moved_re, moved_im, cosine, sine)
    factor = jnp.where(upper, -1.0, 1.0)
    return (base_re + factor * turned_re, base_im + factor * turned_im)


def local_dft(real_part, imag_part, rows_dev, sign):
    index = jnp.arange(rows_dev, dtype=jnp.int32)
    angles = unit_angle(index[:, None] * index[None, :] % rows_dev, rows_dev)
    cosine = jnp.cos(angles)
    sine = sign * jnp.sin(angles)

    def apply_matrix(matrix, data):
        return jnp.einsum("km,emc->ekc", matrix, data, precision=highest)

    new_re = apply_matrix(cosine, real_part) - apply_matrix(sine, imag_part)
    new_im = apply_matrix(cosine, imag_part) + apply_matrix(sine, real_part)
    return (new_re, new_im)


def butterfly_conv(mixed, bank, groups):
    rows_dev, channels = mixed.shape
    devices = lax.axis_size("seq")
    length = rows_dev * devices
    bit_count = devices.bit_length() - 1
    device = lax.axis_index("seq")
    top_level = bit_count - 1
    partner_mixed = swapped(mixed, "seq", top_level)
    current = expand_pair(mixed, device, rows_dev, length)
    partner = expand_pair(partner_mixed, jnp.bitwise_xor(device, 1 << top_level), rows_dev, length)
    state = forward_section(current, partner, device, top_level, rows_dev)
    for level in range(top_level - 1, -1, -1):
        received = swapped(shortened(jnp.stack(state)), "seq", level)
        state = forward_section(state, (received[0], received[1]), device, level, rows_dev)
    spec_re, spec_im = local_dft(state[0], state[1], rows_dev, -1.0)
    residue = jnp.zeros((), jnp.int32)
    for level in range(bit_count):
        residue = residue + ((device >> level & 1) << bit_count - 1 - level)
    freq_even = 2 * (residue + devices * jnp.arange(rows_dev, dtype=jnp.int32))
    freqs = jnp.concatenate([freq_even, freq_even + 1])
    lags = jnp.arange(length, dtype=jnp.int32)
    angles = unit_angle(lags[:, None] * freqs[None, :] % (2 * length), 2 * length)
    table_re = jnp.dot(bank, jnp.cos(angles), precision=highest)
    table_im = -jnp.dot(bank, jnp.sin(angles), precision=highest)
    chosen_re = jnp.take(table_re, groups, axis=0).T.reshape(2, rows_dev, channels)
    chosen_im = jnp.take(table_im, groups, axis=0).T.reshape(2, rows_dev, channels)
    prod_re, prod_im = twist(spec_re, spec_im, chosen_re, chosen_im)
    state = local_dft(prod_re, prod_im, rows_dev, 1.0)
    for level in range(bit_count):
        received = swapped(shortened(jnp.stack(state)), "seq", level)
        state = inverse_section(state, (received[0], received[1]), device, level, rows_dev)
    positions = device * rows_dev + jnp.arange(rows_dev, dtype=jnp.int32)
    final_angles = math.pi / length * positions.astype(jnp.float32)
    cosine = jnp.cos(final_angles)[:, None]
    sine = jnp.sin(final_angles)[:, None]
    return (state[0][0] + cosine * state[0][1] - sine * state[1][1]) / (2.0 * length)


def attention(att_queries, att_keys, hyena_out, block_mask):
    rows_dev, channels = att_queries.shape
    head_count = channels // HD
    device = lax.axis_index("seq")
    block_count = block_mask.shape[1]
    queries = att_queries.reshape(rows_dev, head_count, HD)
    mask_rows = jnp.repeat(block_mask, ABLK, axis=0).astype(jnp.float32)
    query_pos = device * rows_dev + jnp.arange(rows_dev, dtype=jnp.int32)
    scale = HD ** (-0.5)
    key_piece = lax.all_gather(att_keys, "seq", axis=0, tiled=True)
    value_piece = lax.all_gather(hyena_out, "seq", axis=0, tiled=True)
    piece_rows = key_piece.shape[0]
    key_pos = jnp.arange(piece_rows, dtype=jnp.int32)
    onehot = (
        jnp.arange(block_count, dtype=jnp.int32)[:, None] == (key_pos // ABLK)[None, :]
    ).astype(jnp.float32)
    allowed = (jnp.dot(mask_rows, onehot, preferred_element_type=jnp.float32) > 0.5) & (
        key_pos[None, :] <= query_pos[:, None]
    )
    keys_here = key_piece.reshape(piece_rows, head_count, HD)
    values_here = value_piece.reshape(piece_rows, head_count, HD)
    scores = (
        jnp.einsum("thd,shd->hts", queries, keys_here, preferred_element_type=jnp.float32) * scale
    )
    scores = jnp.where(allowed[None], scores, -1e30)
    old_max = jnp.full((head_count, rows_dev), -1e30, jnp.float32)
    new_max = jnp.maximum(old_max, jnp.max(scores, axis=-1))
    weights = jnp.where(allowed[None], jnp.exp(scores - new_max[..., None]), 0.0)
    new_total = jnp.sum(weights, axis=-1)
    new_acc = jnp.einsum(
        "hts,shd->htd",
        weights.astype(jnp.bfloat16),
        values_here,
        preferred_element_type=jnp.float32,
    )
    result = new_acc / new_total[..., None]
    return result.transpose(1, 0, 2).reshape(rows_dev, channels).astype(jnp.bfloat16)


def on_device(
    hyena_query, hyena_key, hyena_value, bias, groups, filters, att_queries, att_keys, block_mask
):
    mixed = (hyena_key.astype(jnp.float32) * hyena_value.astype(jnp.float32)).astype(jnp.bfloat16)
    bank = lax.all_gather(filters.astype(jnp.bfloat16), "chan", axis=0, tiled=True).astype(
        filters.dtype
    )
    bank = lax.all_gather(bank.astype(jnp.bfloat16), "seq", axis=1, tiled=True).astype(bank.dtype)
    conv = butterfly_conv(mixed, bank, groups)
    hyena_out = (
        hyena_query.astype(jnp.float32) * (conv + bias[None, :] * mixed.astype(jnp.float32))
    ).astype(jnp.bfloat16)
    attn_out = attention(att_queries, att_keys, hyena_out, block_mask)
    return (hyena_out, attn_out)


MIXED, GATE, QUERY, KEY, HYENA, ATTN, MASK = range(7)


def half_step_dft(block):
    freqs = np.concatenate([np.arange(0, block, 2), np.arange(1, block, 2)])
    steps = (2 * freqs[:, None] + 1) * np.arange(block)[None, :] % (4 * block)
    angles = steps * (math.pi / (2 * block))
    forward = np.concatenate([np.cos(angles), -np.sin(angles)], axis=0)
    inverse = forward.T / block
    return forward.astype(ml_dtypes.bfloat16), inverse.astype(ml_dtypes.bfloat16)


def fused_kernel(
    n, m,
    hk_far, hv_far, fil_far, grp_far, bias_far, mask_far, fwd_far, inv_far, hq, aq, ak,
    hy, at,
    hk, hv, fil, grp, bias, mask, fwd, inv,
    mixed, select, bank, hot, masks, mixed_in, select_in, gate_in, query_in, key_in,
    values, result, mask_add, spec, fspec,
    lag_send, lag_recv, bank_send, bank_recv, pair_send, pair_recv, send, recv, local, loads,
):
    me = lax.axis_index("seq")
    plane = lax.axis_index("chan")
    side = lax.rem(me, 2)
    sibling = me + 1 - 2 * side
    pair = lax.div(me, 2)
    pairs = n // 2
    rows = hk.shape[0]
    wide = hk.shape[1] // n
    subs = rows // ABLK
    heads = wide // HD
    bf16, f32 = jnp.bfloat16, jnp.float32

    barrier = pltpu.get_barrier_semaphore()
    for d in range(1, n):
        pl.semaphore_signal(
            barrier, inc=1, device_id={"seq": lax.rem(me + d, n)},
            device_id_type=pl.DeviceIdType.MESH,
        )
    for d in range(1, m):
        pl.semaphore_signal(
            barrier, inc=1, device_id={"chan": lax.rem(plane + d, m)},
            device_id_type=pl.DeviceIdType.MESH,
        )

    def columns(p):
        return pl.ds(pl.multiple_of(p * wide, wide), wide)

    def seq_copy(kind, d, src, dst):
        return pltpu.make_async_remote_copy(
            src_ref=src, dst_ref=dst, send_sem=send.at[kind, d], recv_sem=recv.at[kind, d],
            device_id={"seq": lax.rem(me + d, n)}, device_id_type=pl.DeviceIdType.MESH,
        )

    def lag_copy(e):
        return pltpu.make_async_remote_copy(
            src_ref=bank.at[plane, pair], dst_ref=bank.at[plane, pair],
            send_sem=lag_send.at[e], recv_sem=lag_recv.at[e],
            device_id={"seq": lax.rem(me + 2 * e, n)}, device_id_type=pl.DeviceIdType.MESH,
        )

    def bank_copy(e, d):
        part = lax.rem(pair + pairs - e, pairs)
        return pltpu.make_async_remote_copy(
            src_ref=bank.at[plane, part], dst_ref=bank.at[plane, part],
            send_sem=bank_send.at[e, d], recv_sem=bank_recv.at[e, d],
            device_id={"chan": lax.rem(plane + d, m)}, device_id_type=pl.DeviceIdType.MESH,
        )

    def pair_copy(e):
        part = 2 * lax.rem(pair + pairs - e, pairs) + side
        return pltpu.make_async_remote_copy(
            src_ref=select.at[e], dst_ref=select_in.at[part],
            send_sem=pair_send.at[e], recv_sem=pair_recv.at[e],
            device_id={"seq": sibling}, device_id_type=pl.DeviceIdType.MESH,
        )

    def mixed_copy(d):
        return seq_copy(MIXED, d, mixed.at[lax.rem(me + d, n)], mixed_in.at[me])

    def gate_copy(d):
        return seq_copy(GATE, d, hq.at[:, columns(lax.rem(me + d, n))], gate_in.at[me])

    def query_copy(d):
        return seq_copy(QUERY, d, aq.at[:, columns(lax.rem(me + d, n))], query_in.at[me])

    def key_copy(d):
        return seq_copy(KEY, d, ak.at[:, columns(lax.rem(me + d, n))], key_in.at[me])

    def hyena_copy(d):
        return seq_copy(HYENA, d, values.at[lax.rem(me + d, n)], hy.at[:, columns(me)])

    def attn_copy(d):
        return seq_copy(ATTN, d, result.at[lax.rem(me + d, n)], at.at[:, columns(me)])

    def mask_copy(d):
        return seq_copy(MASK, d, masks.at[me], masks.at[me])

    own_in = [
        pltpu.make_async_copy(src.at[:, columns(me)], dst.at[me], local.at[i])
        for i, (src, dst) in enumerate([(hq, gate_in), (aq, query_in), (ak, key_in)])
    ]
    for copy in own_in:
        copy.start()

    near = [
        pltpu.make_async_copy(src, dst, loads.at[i])
        for i, (src, dst) in enumerate([
            (fil_far, fil), (mask_far, mask), (hk_far, hk), (hv_far, hv),
            (grp_far, grp), (fwd_far, fwd), (inv_far, inv), (bias_far, bias),
        ])
    ]
    for copy in near:
        copy.start()

    near[0].wait()
    near[1].wait()
    bank[plane, pair] = fil[...].T.astype(bf16)
    masks[me] = jnp.zeros(masks.shape[1:], f32)
    masks[me, 0:subs, 0 : mask.shape[1]] = mask[...].astype(f32)
    near[2].wait()
    near[3].wait()
    for p in range(n):
        part = slice(p * wide, (p + 1) * wide)
        mixed[p] = (hk[:, part].astype(f32) * hv[:, part].astype(f32)).astype(bf16)

    pl.semaphore_wait(barrier, n + m - 2)
    for e in range(1, pairs):
        lag_copy(e).start()
    for d in range(1, m):
        bank_copy(0, d).start()
    for d in range(1, n):
        mixed_copy(d).start()
    for d in range(1, n):
        mask_copy(d).start()

    mixed_in[me] = mixed[me]
    near[4].wait()
    lanes_here = bank.shape[3]
    for which, owner in enumerate((me, sibling)):
        index = lax.broadcasted_iota(jnp.int32, (m * lanes_here, wide), 0)
        hot[which] = jnp.where(index == grp[owner], 1.0, 0.0).astype(bf16)

    for e in range(1, pairs):
        lag_copy(e).wait()
        for d in range(1, m):
            bank_copy(e, d).start()

    near[5].wait()
    spec[me] = jnp.dot(fwd[...], mixed_in[me], preferred_element_type=f32)

    def signal_step(d, carry):
        mixed_copy(d).wait()
        i = lax.rem(me + n - d, n)
        spec[i] = jnp.dot(fwd[...], mixed_in[i], preferred_element_type=f32)
        return carry

    lax.fori_loop(1, n // 2 + 1, signal_step, 0)
    for d in range(1, n):
        gate_copy(d).start()
    lax.fori_loop(n // 2 + 1, n, signal_step, 0)

    def chosen(part, which):
        table = jnp.concatenate([bank[k, part] for k in range(m)], axis=1)
        return jnp.dot(table, hot[which], preferred_element_type=f32).astype(bf16)

    for e in range(pairs):
        for d in range(1, m):
            bank_copy(e, d).wait()
        part = lax.rem(pair + pairs - e, pairs)
        select[e] = chosen(part, 1)
        pair_copy(e).start()
        own = 2 * part + side
        fspec[own] = jnp.dot(fwd[...], chosen(part, 0), preferred_element_type=f32)
        if e == 0:
            for d in range(1, n):
                query_copy(d).start()
        if e == min(1, pairs - 1):
            for d in range(1, n):
                key_copy(d).start()
    for e in range(pairs):
        pair_copy(e).wait()
        other = 2 * lax.rem(pair + pairs - e, pairs) + 1 - side
        fspec[other] = jnp.dot(fwd[...], select_in[other], preferred_element_type=f32)

    tiles = rows // 8

    def product(t, carry):
        re = pl.ds(pl.multiple_of(t * 8, 8), 8)
        im = pl.ds(pl.multiple_of(rows + t * 8, 8), 8)
        turn = jnp.where(t < tiles // 2, 1.0, -1.0).astype(f32)
        for lane in range(0, wide, 128):
            lanes = slice(lane, lane + 128)
            xr = [spec[i, re, lanes] for i in range(n)]
            xi = [spec[i, im, lanes] for i in range(n)]
            gr = [fspec[i, re, lanes] for i in range(n)]
            gi = [fspec[i, im, lanes] for i in range(n)]
            last_re = last_im = None
            for j in range(n):
                sum_re = sum_im = None
                for i in range(j + 1):
                    a, b, c, e = xr[i], xi[i], gr[j - i], gi[j - i]
                    new_re, new_im = a * c - b * e, a * e + b * c
                    sum_re = new_re if sum_re is None else sum_re + new_re
                    sum_im = new_im if sum_im is None else sum_im + new_im
                if j == 0:
                    spec[j, re, lanes] = sum_re
                    spec[j, im, lanes] = sum_im
                else:
                    spec[j, re, lanes] = sum_re - turn * last_im
                    spec[j, im, lanes] = sum_im + turn * last_re
                last_re, last_im = sum_re, sum_im
        return carry

    lax.fori_loop(0, tiles, product, 0)

    own_in[0].wait()
    near[6].wait()
    near[7].wait()

    def finish(j):
        conv = jnp.dot(inv[...], spec[j].astype(bf16), preferred_element_type=f32)
        direct = bias[me] * mixed_in[j].astype(f32)
        values[j] = (gate_in[j].astype(f32) * (conv + direct)).astype(bf16)

    def hyena_step(d, carry):
        gate_copy(n - d).wait()
        finish(lax.rem(me + d, n))
        return carry

    lax.fori_loop(1, n, hyena_step, 0)
    finish(me)
    own_hyena = pltpu.make_async_copy(values.at[me], hy.at[:, columns(me)], local.at[3])
    own_hyena.start()

    for d in range(1, n):
        mask_copy(d).wait()
    flags = masks[...].reshape(n * masks.shape[1], masks.shape[2]).astype(bf16)
    for k in range(n):
        block_id = lax.broadcasted_iota(jnp.int32, (masks.shape[2], rows), 0)
        owner = lax.broadcasted_iota(jnp.int32, (masks.shape[2], rows), 1) // ABLK + k * subs
        spread = jnp.where(block_id == owner, 1.0, 0.0).astype(bf16)
        shown = jnp.dot(flags, spread, preferred_element_type=f32)
        mask_add[:, k] = ((shown - 1.0) * 1e30).reshape(n, masks.shape[1], rows)

    own_in[1].wait()
    own_in[2].wait()
    for d in range(1, n):
        query_copy(d).wait()
    for d in range(1, n // 2 + 1):
        key_copy(d).wait()
    for d in range(1, n):
        hyena_copy(d).start()
    for d in range(n // 2 + 1, n):
        key_copy(d).wait()
    scale = HD ** (-0.5) / math.log(2.0)

    def lane_sum(weights):
        total = weights[:, 0:128]
        for lane in range(128, rows, 128):
            total = total + weights[:, lane : lane + 128]
        return total

    def attend(r):

        def scores(h, k):
            part = slice(h * HD, (h + 1) * HD)
            return lax.dot_general(
                query_in[r, :, part], key_in[k, :, part], (((1,), (1,)), ((), ())),
                preferred_element_type=f32,
            )

        def weighted(h, k, weights):
            part = slice(h * HD, (h + 1) * HD)
            return jnp.dot(weights.astype(bf16), values[k, :, part], preferred_element_type=f32)

        def added(k):
            flags_here = mask_add[r, k]
            return jnp.concatenate(
                [jnp.broadcast_to(flags_here[i : i + 1], (ABLK, rows)) for i in range(subs)], axis=0
            )

        row = lax.broadcasted_iota(jnp.int32, (rows, rows), 0)
        col = lax.broadcasted_iota(jnp.int32, (rows, rows), 1)
        add = jnp.where(col <= row, added(r), -1e30)
        state = []
        for h in range(heads):
            here = scores(h, r) + add
            top = jnp.max(here, axis=1, keepdims=True)
            weights = jnp.exp2((here - top) * scale)
            state.append((top, lane_sum(weights), weighted(h, r, weights), scores(h, 0)))

        def step(k, state):
            add = added(k)
            out = []
            for h in range(heads):
                top, total, acc, raw = state[h]
                ahead = scores(h, k + 1)
                here = raw + add
                new_top = jnp.maximum(top, jnp.max(here, axis=1, keepdims=True))
                weights = jnp.exp2((here - new_top) * scale)
                keep = jnp.exp2((top - new_top) * scale)
                total = total * keep + lane_sum(weights)
                out.append((new_top, total, acc * keep + weighted(h, k, weights), ahead))
            return tuple(out)

        state = lax.fori_loop(0, r, step, tuple(state))
        for h in range(heads):
            total = jnp.sum(state[h][1], axis=1, keepdims=True)
            result[r, :, h * HD : (h + 1) * HD] = (state[h][2] / total).astype(bf16)

    def attn_step(d, carry):
        attend(lax.rem(me + d, n))
        attn_copy(d).start()
        return carry

    lax.fori_loop(1, n, attn_step, 0)
    attend(me)
    own_attn = pltpu.make_async_copy(result.at[me], at.at[:, columns(me)], local.at[4])
    own_attn.start()
    own_hyena.wait()
    own_attn.wait()
    for d in range(1, n):
        hyena_copy(d).wait()
    for d in range(1, n):
        attn_copy(d).wait()


def copy_kernel(parts, hy, at, hy_out, at_out, held, load, store):
    step = hy.shape[0] // parts
    loads, stores = [], []
    for i, (src, dst) in enumerate([(hy, hy_out), (at, at_out)]):
        for k in range(parts):
            part = pl.ds(k * step, step)
            loads.append(pltpu.make_async_copy(src.at[part], held.at[i, part], load.at[i, k]))
            stores.append(pltpu.make_async_copy(held.at[i, part], dst.at[part], store.at[i, k]))
    for copy in loads:
        copy.start()
    for first, second in zip(loads, stores):
        first.wait()
        second.start()
    for copy in stores:
        copy.wait()


def fused_on_device(
    n, m, hyena_query, hyena_key, hyena_value, bias, groups, filters, att_queries, att_keys, block_mask
):
    rows, channels = hyena_key.shape
    wide = channels // n
    lanes = filters.shape[0]
    pairs = n // 2
    forward, inverse = half_step_dft(rows)
    bf16, f32 = jnp.bfloat16, jnp.float32
    blocks = pltpu.VMEM((n, rows, wide), bf16)
    anywhere = pl.BlockSpec(memory_space=pl.ANY)
    dma = pltpu.SemaphoreType.DMA
    outs = [jax.ShapeDtypeStruct((rows, channels), bf16)] * 2
    hyena_out, attn_out = pl.pallas_call(
        functools.partial(fused_kernel, n, m),
        out_shape=outs,
        in_specs=[anywhere] * 11,
        out_specs=[anywhere] * 2,
        scratch_shapes=[
            pltpu.VMEM((rows, channels), bf16),
            pltpu.VMEM((rows, channels), bf16),
            pltpu.VMEM(filters.shape, f32),
            pltpu.VMEM((n, 1, wide), jnp.int32),
            pltpu.VMEM((n, 1, wide), f32),
            pltpu.VMEM(block_mask.shape, jnp.int32),
            pltpu.VMEM(forward.shape, bf16),
            pltpu.VMEM(inverse.shape, bf16),
            blocks,
            pltpu.VMEM((pairs, rows, wide), bf16),
            pltpu.VMEM((m, pairs, rows, lanes), bf16),
            pltpu.VMEM((2, m * lanes, wide), bf16),
            pltpu.VMEM((n, 8, 128), f32),
            blocks,
            blocks,
            blocks,
            blocks,
            blocks,
            blocks,
            blocks,
            pltpu.VMEM((n, n, 8, rows), f32),
            pltpu.VMEM((n, 2 * rows, wide), f32),
            pltpu.VMEM((n, 2 * rows, wide), f32),
            dma((pairs,)),
            dma((pairs,)),
            dma((pairs, m)),
            dma((pairs, m)),
            dma((pairs,)),
            dma((pairs,)),
            dma((7, n)),
            dma((7, n)),
            dma((5,)),
            dma((8,)),
        ],
        compiler_params=pltpu.CompilerParams(
            collective_id=0, has_side_effects=True, vmem_limit_bytes=60 * 1024 * 1024
        ),
        name="hyena_attention",
    )(
        hyena_key, hyena_value, filters,
        groups.reshape(n, 1, wide), bias.reshape(n, 1, wide), block_mask,
        jnp.asarray(forward), jnp.asarray(inverse),
        hyena_query, att_queries, att_keys,
    )
    parts = 4
    return pl.pallas_call(
        functools.partial(copy_kernel, parts),
        out_shape=outs,
        in_specs=[anywhere] * 2,
        out_specs=[anywhere] * 2,
        scratch_shapes=[pltpu.VMEM((2, rows, channels), bf16), dma((2, parts)), dma((2, parts))],
        compiler_params=pltpu.CompilerParams(vmem_limit_bytes=60 * 1024 * 1024),
        name="results",
    )(hyena_out, attn_out)


def by_shape(
    n, m, hyena_query, hyena_key, hyena_value, bias, groups, filters, att_queries, att_keys, block_mask
):
    rows, channels = hyena_key.shape
    fits = (
        channels % (n * HD) == 0
        and n % 2 == 0
        and rows % (2 * ABLK) == 0
        and rows // ABLK <= 8
        and block_mask.shape[1] <= 128
        and filters.shape[0] % 128 == 0
        and filters.shape[1] == rows
    )
    args = (
        hyena_query, hyena_key, hyena_value, bias, groups, filters, att_queries, att_keys, block_mask
    )
    return fused_on_device(n, m, *args) if fits else on_device(*args)


def solution(mesh):
    return jax.shard_map(
        functools.partial(by_shape, mesh.shape["seq"], mesh.shape["chan"]),
        mesh=mesh,
        in_specs=(
            P("seq", "chan"),
            P("seq", "chan"),
            P("seq", "chan"),
            P("chan"),
            P("chan"),
            P("chan", "seq"),
            P("seq", "chan"),
            P("seq", "chan"),
            P("seq", None),
        ),
        out_specs=(P("seq", "chan"), P("seq", "chan")),
        check_vma=False,
    )
```

```python
import functools
import math

import jax
import jax.numpy as jnp
import ml_dtypes
import numpy as np
from jax import lax
from jax.experimental import pallas as pl
from jax.experimental.pallas import tpu as pltpu
from jax.sharding import PartitionSpec as P

HD = 128
ABLK = 128


highest = lax.Precision.HIGHEST


def swapped(value, axis, stride):
    mask = 2**stride
    pairs = [(source, source ^ mask) for source in range(lax.axis_size(axis))]
    return lax.ppermute(value, axis, pairs)


def shortened(x):

    def short(part):
        return part.astype(jnp.bfloat16) if part.dtype == jnp.float32 else part

    return jax.tree.map(short, x)


def unit_angle(numer, denom):
    return 2.0 * math.pi / denom * numer.astype(jnp.float32)


def twist(real_part, imag_part, cosine, sine):
    return (real_part * cosine - imag_part * sine, real_part * sine + imag_part * cosine)


def expand_pair(signal, device, rows_dev, length):
    positions = device * rows_dev + jnp.arange(rows_dev, dtype=jnp.int32)
    angles = math.pi / length * positions.astype(jnp.float32)
    values = signal.astype(jnp.float32)
    cosine = jnp.cos(angles)[:, None]
    sine = jnp.sin(angles)[:, None]
    real_part = jnp.stack([values, values * cosine])
    imag_part = jnp.stack([jnp.zeros_like(values), -values * sine])
    return (real_part, imag_part)


def section_twiddle(device, level, rows_dev, sign):
    inner = device % (1 << level) * rows_dev + jnp.arange(rows_dev, dtype=jnp.int32)
    angles = unit_angle(inner, rows_dev << level + 1)
    return (jnp.cos(angles)[:, None], sign * jnp.sin(angles)[:, None])


def forward_section(current, partner, device, level, rows_dev):
    cosine, sine = section_twiddle(device, level, rows_dev, -1.0)
    upper = device >> level & 1 == 1
    diff_re = partner[0] - current[0]
    diff_im = partner[1] - current[1]
    turned_re, turned_im = twist(diff_re, diff_im, cosine, sine)
    return (
        jnp.where(upper, turned_re, current[0] + partner[0]),
        jnp.where(upper, turned_im, current[1] + partner[1]),
    )


def inverse_section(current, partner, device, level, rows_dev):
    cosine, sine = section_twiddle(device, level, rows_dev, 1.0)
    upper = device >> level & 1 == 1
    moved_re = jnp.where(upper, current[0], partner[0])
    moved_im = jnp.where(upper, current[1], partner[1])
    base_re = jnp.where(upper, partner[0], current[0])
    base_im = jnp.where(upper, partner[1], current[1])
    turned_re, turned_im = twist(moved_re, moved_im, cosine, sine)
    factor = jnp.where(upper, -1.0, 1.0)
    return (base_re + factor * turned_re, base_im + factor * turned_im)


def local_dft(real_part, imag_part, rows_dev, sign):
    index = jnp.arange(rows_dev, dtype=jnp.int32)
    angles = unit_angle(index[:, None] * index[None, :] % rows_dev, rows_dev)
    cosine = jnp.cos(angles)
    sine = sign * jnp.sin(angles)

    def apply_matrix(matrix, data):
        return jnp.einsum("km,emc->ekc", matrix, data, precision=highest)

    new_re = apply_matrix(cosine, real_part) - apply_matrix(sine, imag_part)
    new_im = apply_matrix(cosine, imag_part) + apply_matrix(sine, real_part)
    return (new_re, new_im)


def butterfly_conv(mixed, bank, groups):
    rows_dev, channels = mixed.shape
    devices = lax.axis_size("seq")
    length = rows_dev * devices
    bit_count = devices.bit_length() - 1
    device = lax.axis_index("seq")
    top_level = bit_count - 1
    partner_mixed = swapped(mixed, "seq", top_level)
    current = expand_pair(mixed, device, rows_dev, length)
    partner = expand_pair(partner_mixed, jnp.bitwise_xor(device, 1 << top_level), rows_dev, length)
    state = forward_section(current, partner, device, top_level, rows_dev)
    for level in range(top_level - 1, -1, -1):
        received = swapped(shortened(jnp.stack(state)), "seq", level)
        state = forward_section(state, (received[0], received[1]), device, level, rows_dev)
    spec_re, spec_im = local_dft(state[0], state[1], rows_dev, -1.0)
    residue = jnp.zeros((), jnp.int32)
    for level in range(bit_count):
        residue = residue + ((device >> level & 1) << bit_count - 1 - level)
    freq_even = 2 * (residue + devices * jnp.arange(rows_dev, dtype=jnp.int32))
    freqs = jnp.concatenate([freq_even, freq_even + 1])
    lags = jnp.arange(length, dtype=jnp.int32)
    angles = unit_angle(lags[:, None] * freqs[None, :] % (2 * length), 2 * length)
    table_re = jnp.dot(bank, jnp.cos(angles), precision=highest)
    table_im = -jnp.dot(bank, jnp.sin(angles), precision=highest)
    chosen_re = jnp.take(table_re, groups, axis=0).T.reshape(2, rows_dev, channels)
    chosen_im = jnp.take(table_im, groups, axis=0).T.reshape(2, rows_dev, channels)
    prod_re, prod_im = twist(spec_re, spec_im, chosen_re, chosen_im)
    state = local_dft(prod_re, prod_im, rows_dev, 1.0)
    for level in range(bit_count):
        received = swapped(shortened(jnp.stack(state)), "seq", level)
        state = inverse_section(state, (received[0], received[1]), device, level, rows_dev)
    positions = device * rows_dev + jnp.arange(rows_dev, dtype=jnp.int32)
    final_angles = math.pi / length * positions.astype(jnp.float32)
    cosine = jnp.cos(final_angles)[:, None]
    sine = jnp.sin(final_angles)[:, None]
    return (state[0][0] + cosine * state[0][1] - sine * state[1][1]) / (2.0 * length)


def attention(att_queries, att_keys, hyena_out, block_mask):
    rows_dev, channels = att_queries.shape
    head_count = channels // HD
    device = lax.axis_index("seq")
    block_count = block_mask.shape[1]
    queries = att_queries.reshape(rows_dev, head_count, HD)
    mask_rows = jnp.repeat(block_mask, ABLK, axis=0).astype(jnp.float32)
    query_pos = device * rows_dev + jnp.arange(rows_dev, dtype=jnp.int32)
    scale = HD ** (-0.5)
    key_piece = lax.all_gather(att_keys, "seq", axis=0, tiled=True)
    value_piece = lax.all_gather(hyena_out, "seq", axis=0, tiled=True)
    piece_rows = key_piece.shape[0]
    key_pos = jnp.arange(piece_rows, dtype=jnp.int32)
    onehot = (
        jnp.arange(block_count, dtype=jnp.int32)[:, None] == (key_pos // ABLK)[None, :]
    ).astype(jnp.float32)
    allowed = (jnp.dot(mask_rows, onehot, preferred_element_type=jnp.float32) > 0.5) & (
        key_pos[None, :] <= query_pos[:, None]
    )
    keys_here = key_piece.reshape(piece_rows, head_count, HD)
    values_here = value_piece.reshape(piece_rows, head_count, HD)
    scores = (
        jnp.einsum("thd,shd->hts", queries, keys_here, preferred_element_type=jnp.float32) * scale
    )
    scores = jnp.where(allowed[None], scores, -1e30)
    old_max = jnp.full((head_count, rows_dev), -1e30, jnp.float32)
    new_max = jnp.maximum(old_max, jnp.max(scores, axis=-1))
    weights = jnp.where(allowed[None], jnp.exp(scores - new_max[..., None]), 0.0)
    new_total = jnp.sum(weights, axis=-1)
    new_acc = jnp.einsum(
        "hts,shd->htd",
        weights.astype(jnp.bfloat16),
        values_here,
        preferred_element_type=jnp.float32,
    )
    result = new_acc / new_total[..., None]
    return result.transpose(1, 0, 2).reshape(rows_dev, channels).astype(jnp.bfloat16)


def on_device(
    hyena_query, hyena_key, hyena_value, bias, groups, filters, att_queries, att_keys, block_mask
):
    mixed = (hyena_key.astype(jnp.float32) * hyena_value.astype(jnp.float32)).astype(jnp.bfloat16)
    bank = lax.all_gather(filters.astype(jnp.bfloat16), "chan", axis=0, tiled=True).astype(
        filters.dtype
    )
    bank = lax.all_gather(bank.astype(jnp.bfloat16), "seq", axis=1, tiled=True).astype(bank.dtype)
    conv = butterfly_conv(mixed, bank, groups)
    hyena_out = (
        hyena_query.astype(jnp.float32) * (conv + bias[None, :] * mixed.astype(jnp.float32))
    ).astype(jnp.bfloat16)
    attn_out = attention(att_queries, att_keys, hyena_out, block_mask)
    return (hyena_out, attn_out)


MIXED, GATE, QUERY, KEY, HYENA, ATTN, MASK = range(7)


def half_step_dft(block):
    freqs = np.concatenate([np.arange(0, block, 2), np.arange(1, block, 2)])
    steps = (2 * freqs[:, None] + 1) * np.arange(block)[None, :] % (4 * block)
    angles = steps * (math.pi / (2 * block))
    forward = np.concatenate([np.cos(angles), -np.sin(angles)], axis=0)
    inverse = forward.T / block
    return forward.astype(ml_dtypes.bfloat16), inverse.astype(ml_dtypes.bfloat16)


def fused_kernel(
    n, m,
    hk_far, hv_far, fil_far, grp_far, bias_far, mask_far, fwd_far, inv_far, hq, aq, ak,
    hy, at,
    hk, hv, fil, grp, bias, mask, fwd, inv,
    mixed, select, bank, hot, masks, mixed_in, select_in, gate_in, query_in, key_in,
    values, result, mask_add, spec, fspec, scored, weighed, totals,
    lag_send, lag_recv, bank_send, bank_recv, pair_send, pair_recv, send, recv, local, loads,
):
    me = lax.axis_index("seq")
    plane = lax.axis_index("chan")
    side = lax.rem(me, 2)
    sibling = me + 1 - 2 * side
    pair = lax.div(me, 2)
    pairs = n // 2
    rows = hk.shape[0]
    wide = hk.shape[1] // n
    subs = rows // ABLK
    heads = wide // HD
    bf16, f32 = jnp.bfloat16, jnp.float32

    barrier = pltpu.get_barrier_semaphore()
    for d in range(1, n):
        pl.semaphore_signal(
            barrier, inc=1, device_id={"seq": lax.rem(me + d, n)},
            device_id_type=pl.DeviceIdType.MESH,
        )
    for d in range(1, m):
        pl.semaphore_signal(
            barrier, inc=1, device_id={"chan": lax.rem(plane + d, m)},
            device_id_type=pl.DeviceIdType.MESH,
        )

    def columns(p):
        return pl.ds(pl.multiple_of(p * wide, wide), wide)

    def seq_copy(kind, d, src, dst):
        return pltpu.make_async_remote_copy(
            src_ref=src, dst_ref=dst, send_sem=send.at[kind, d], recv_sem=recv.at[kind, d],
            device_id={"seq": lax.rem(me + d, n)}, device_id_type=pl.DeviceIdType.MESH,
        )

    def lag_copy(e):
        return pltpu.make_async_remote_copy(
            src_ref=bank.at[plane, pair], dst_ref=bank.at[plane, pair],
            send_sem=lag_send.at[e], recv_sem=lag_recv.at[e],
            device_id={"seq": lax.rem(me + 2 * e, n)}, device_id_type=pl.DeviceIdType.MESH,
        )

    def bank_copy(e, d):
        part = lax.rem(pair + pairs - e, pairs)
        return pltpu.make_async_remote_copy(
            src_ref=bank.at[plane, part], dst_ref=bank.at[plane, part],
            send_sem=bank_send.at[e, d], recv_sem=bank_recv.at[e, d],
            device_id={"chan": lax.rem(plane + d, m)}, device_id_type=pl.DeviceIdType.MESH,
        )

    def pair_copy(e):
        part = 2 * lax.rem(pair + pairs - e, pairs) + side
        return pltpu.make_async_remote_copy(
            src_ref=select.at[e], dst_ref=select_in.at[part],
            send_sem=pair_send.at[e], recv_sem=pair_recv.at[e],
            device_id={"seq": sibling}, device_id_type=pl.DeviceIdType.MESH,
        )

    def mixed_copy(d):
        return seq_copy(MIXED, d, mixed.at[lax.rem(me + d, n)], mixed_in.at[me])

    def gate_copy(d):
        return seq_copy(GATE, d, hq.at[:, columns(lax.rem(me + d, n))], gate_in.at[me])

    def query_copy(d):
        return seq_copy(QUERY, d, aq.at[:, columns(lax.rem(me + d, n))], query_in.at[me])

    def key_copy(d):
        return seq_copy(KEY, d, ak.at[:, columns(lax.rem(me + d, n))], key_in.at[me])

    def hyena_copy(d):
        return seq_copy(HYENA, d, values.at[lax.rem(me + d, n)], hy.at[:, columns(me)])

    def attn_copy(d):
        return seq_copy(ATTN, d, result.at[lax.rem(me + d, n)], at.at[:, columns(me)])

    def mask_copy(d):
        return seq_copy(MASK, d, masks.at[me], masks.at[me])

    own_in = [
        pltpu.make_async_copy(src.at[:, columns(me)], dst.at[me], local.at[i])
        for i, (src, dst) in enumerate([(hq, gate_in), (aq, query_in), (ak, key_in)])
    ]
    for copy in own_in:
        copy.start()

    near = [
        pltpu.make_async_copy(src, dst, loads.at[i])
        for i, (src, dst) in enumerate([
            (fil_far, fil), (mask_far, mask), (hk_far, hk), (hv_far, hv),
            (grp_far, grp), (fwd_far, fwd), (inv_far, inv), (bias_far, bias),
        ])
    ]
    for copy in near:
        copy.start()

    near[0].wait()
    near[1].wait()
    bank[plane, pair] = fil[...].T.astype(bf16)
    masks[me] = jnp.zeros(masks.shape[1:], f32)
    masks[me, 0:subs, 0 : mask.shape[1]] = mask[...].astype(f32)
    pl.semaphore_wait(barrier, n + m - 2)
    for e in range(1, pairs):
        lag_copy(e).start()
    for d in range(1, m):
        bank_copy(0, d).start()
    for d in range(1, n):
        mask_copy(d).start()
    for d in range(1, n):
        key_copy(d).start()
    for d in range(1, n):
        query_copy(d).start()

    near[2].wait()
    near[3].wait()
    for p in range(n):
        part = slice(p * wide, (p + 1) * wide)
        mixed[p] = (hk[:, part].astype(f32) * hv[:, part].astype(f32)).astype(bf16)
    mixed_in[me] = mixed[me]
    near[4].wait()
    lanes_here = bank.shape[3]
    for which, owner in enumerate((me, sibling)):
        index = lax.broadcasted_iota(jnp.int32, (m * lanes_here, wide), 0)
        hot[which] = jnp.where(index == grp[owner], 1.0, 0.0).astype(bf16)

    for e in range(1, pairs):
        lag_copy(e).wait()
        for d in range(1, m):
            bank_copy(e, d).start()

    for d in range(1, n):
        mask_copy(d).wait()
    flags = masks[...].reshape(n * masks.shape[1], masks.shape[2]).astype(bf16)
    for k in range(n):
        block_id = lax.broadcasted_iota(jnp.int32, (masks.shape[2], rows), 0)
        owner = lax.broadcasted_iota(jnp.int32, (masks.shape[2], rows), 1) // ABLK + k * subs
        spread = jnp.where(block_id == owner, 1.0, 0.0).astype(bf16)
        shown = jnp.dot(flags, spread, preferred_element_type=f32)
        mask_add[:, k] = ((shown - 1.0) * 1e30).reshape(n, masks.shape[1], rows)

    own_in[1].wait()
    own_in[2].wait()
    for d in range(1, n):
        key_copy(d).wait()
    for d in range(1, n):
        mixed_copy(d).start()
    for d in range(1, n):
        query_copy(d).wait()
    for d in range(1, n):
        gate_copy(d).start()
    scale = HD ** (-0.5) / math.log(2.0)

    def over_lanes(op, tile):
        out = tile[:, 0:128]
        for lane in range(128, rows, 128):
            out = op(out, tile[:, lane : lane + 128])
        return out

    def weigh(r, carry):

        def scores(h, k):
            part = slice(h * HD, (h + 1) * HD)
            return lax.dot_general(
                query_in[r, :, part], key_in[k, :, part], (((1,), (1,)), ((), ())),
                preferred_element_type=f32,
            )

        def added(k, more):
            row_flags = mask_add[r, k] + more
            return jnp.concatenate(
                [jnp.broadcast_to(row_flags[i : i + 1], (ABLK, rows)) for i in range(subs)], axis=0
            )

        def score_pair(i, tops):
            tops = list(tops)
            for k in (2 * i, 2 * i + 1):
                add = added(k, jnp.where(k < r, 0.0, -1e30).astype(f32))
                for h in range(heads):
                    here = scores(h, k) + add
                    scored[k, h] = here
                    tops[h] = jnp.maximum(tops[h], over_lanes(jnp.maximum, here))
            return tuple(tops)

        tops = lax.fori_loop(
            0, (r + 1) // 2, score_pair, (jnp.full((rows, 128), -3e30, f32),) * heads
        )
        row = lax.broadcasted_iota(jnp.int32, (rows, rows), 0)
        col = lax.broadcasted_iota(jnp.int32, (rows, rows), 1)
        add = jnp.where(col <= row, added(r, 0.0), -1e30)
        largest = []
        for h in range(heads):
            here = scores(h, r) + add
            scored[r, h] = here
            top = jnp.maximum(tops[h], over_lanes(jnp.maximum, here))
            largest.append(jnp.max(top, axis=1, keepdims=True))

        def weight(k, sums):
            out = []
            for h in range(heads):
                weights = jnp.exp2((scored[k, h] - largest[h]) * scale)
                weighed[r, k, h] = weights.astype(bf16)
                out.append(sums[h] + over_lanes(jnp.add, weights))
            return tuple(out)

        sums = lax.fori_loop(0, r + 1, weight, (jnp.zeros((rows, 128), f32),) * heads)
        for h in range(heads):
            whole = jnp.sum(sums[h], axis=1, keepdims=True)
            totals[r, h] = jnp.broadcast_to(whole, (rows, HD))
        return carry

    lax.fori_loop(0, n, weigh, 0)

    near[5].wait()
    spec[me] = jnp.dot(fwd[...], mixed_in[me], preferred_element_type=f32)

    def signal_step(d, carry):
        mixed_copy(d).wait()
        i = lax.rem(me + n - d, n)
        spec[i] = jnp.dot(fwd[...], mixed_in[i], preferred_element_type=f32)
        return carry

    lax.fori_loop(1, n, signal_step, 0)

    def chosen(part, which):
        table = jnp.concatenate([bank[k, part] for k in range(m)], axis=1)
        return jnp.dot(table, hot[which], preferred_element_type=f32).astype(bf16)

    for e in range(pairs):
        for d in range(1, m):
            bank_copy(e, d).wait()
        part = lax.rem(pair + pairs - e, pairs)
        select[e] = chosen(part, 1)
        pair_copy(e).start()
        own = 2 * part + side
        fspec[own] = jnp.dot(fwd[...], chosen(part, 0), preferred_element_type=f32)
    for e in range(pairs):
        pair_copy(e).wait()
        other = 2 * lax.rem(pair + pairs - e, pairs) + 1 - side
        fspec[other] = jnp.dot(fwd[...], select_in[other], preferred_element_type=f32)

    tiles = rows // 8

    def product(t, carry):
        re = pl.ds(pl.multiple_of(t * 8, 8), 8)
        im = pl.ds(pl.multiple_of(rows + t * 8, 8), 8)
        turn = jnp.where(t < tiles // 2, 1.0, -1.0).astype(f32)
        for lane in range(0, wide, 128):
            lanes = slice(lane, lane + 128)
            xr = [spec[i, re, lanes] for i in range(n)]
            xi = [spec[i, im, lanes] for i in range(n)]
            gr = [fspec[i, re, lanes] for i in range(n)]
            gi = [fspec[i, im, lanes] for i in range(n)]
            last_re = last_im = None
            for j in range(n):
                sum_re = sum_im = None
                for i in range(j + 1):
                    a, b, c, e = xr[i], xi[i], gr[j - i], gi[j - i]
                    new_re, new_im = a * c - b * e, a * e + b * c
                    sum_re = new_re if sum_re is None else sum_re + new_re
                    sum_im = new_im if sum_im is None else sum_im + new_im
                if j == 0:
                    spec[j, re, lanes] = sum_re
                    spec[j, im, lanes] = sum_im
                else:
                    spec[j, re, lanes] = sum_re - turn * last_im
                    spec[j, im, lanes] = sum_im + turn * last_re
                last_re, last_im = sum_re, sum_im
        return carry

    lax.fori_loop(0, tiles, product, 0)

    own_in[0].wait()
    near[6].wait()
    near[7].wait()

    def finish(j):
        conv = jnp.dot(inv[...], spec[j].astype(bf16), preferred_element_type=f32)
        direct = bias[me] * mixed_in[j].astype(f32)
        values[j] = (gate_in[j].astype(f32) * (conv + direct)).astype(bf16)

    def hyena_step(d, carry):
        gate_copy(n - d).wait()
        finish(lax.rem(me + d, n))
        hyena_copy(d).start()
        return carry

    lax.fori_loop(1, n, hyena_step, 0)
    finish(me)
    own_hyena = pltpu.make_async_copy(values.at[me], hy.at[:, columns(me)], local.at[3])
    own_hyena.start()

    def attend(r):

        def step(k, accs):
            return tuple(
                accs[h] + jnp.dot(
                    weighed[r, k, h], values[k, :, h * HD : (h + 1) * HD],
                    preferred_element_type=f32,
                )
                for h in range(heads)
            )

        accs = lax.fori_loop(0, r + 1, step, (jnp.zeros((rows, HD), f32),) * heads)
        for h in range(heads):
            result[r, :, h * HD : (h + 1) * HD] = (accs[h] / totals[r, h]).astype(bf16)

    def attn_step(d, carry):
        attend(lax.rem(me + d, n))
        attn_copy(d).start()
        return carry

    lax.fori_loop(1, n, attn_step, 0)
    attend(me)
    own_attn = pltpu.make_async_copy(result.at[me], at.at[:, columns(me)], local.at[4])
    own_attn.start()
    own_hyena.wait()
    own_attn.wait()
    for d in range(1, n):
        hyena_copy(d).wait()
    for d in range(1, n):
        attn_copy(d).wait()


def copy_kernel(parts, hy, at, hy_out, at_out, held, load, store):
    step = hy.shape[0] // parts
    loads, stores = [], []
    for i, (src, dst) in enumerate([(hy, hy_out), (at, at_out)]):
        for k in range(parts):
            part = pl.ds(k * step, step)
            loads.append(pltpu.make_async_copy(src.at[part], held.at[i, part], load.at[i, k]))
            stores.append(pltpu.make_async_copy(held.at[i, part], dst.at[part], store.at[i, k]))
    for copy in loads:
        copy.start()
    for first, second in zip(loads, stores):
        first.wait()
        second.start()
    for copy in stores:
        copy.wait()


def fused_on_device(
    n, m, hyena_query, hyena_key, hyena_value, bias, groups, filters, att_queries, att_keys, block_mask
):
    rows, channels = hyena_key.shape
    wide = channels // n
    lanes = filters.shape[0]
    pairs = n // 2
    forward, inverse = half_step_dft(rows)
    bf16, f32 = jnp.bfloat16, jnp.float32
    blocks = pltpu.VMEM((n, rows, wide), bf16)
    anywhere = pl.BlockSpec(memory_space=pl.ANY)
    dma = pltpu.SemaphoreType.DMA
    outs = [jax.ShapeDtypeStruct((rows, channels), bf16)] * 2
    hyena_out, attn_out = pl.pallas_call(
        functools.partial(fused_kernel, n, m),
        out_shape=outs,
        in_specs=[anywhere] * 11,
        out_specs=[anywhere] * 2,
        scratch_shapes=[
            pltpu.VMEM((rows, channels), bf16),
            pltpu.VMEM((rows, channels), bf16),
            pltpu.VMEM(filters.shape, f32),
            pltpu.VMEM((n, 1, wide), jnp.int32),
            pltpu.VMEM((n, 1, wide), f32),
            pltpu.VMEM(block_mask.shape, jnp.int32),
            pltpu.VMEM(forward.shape, bf16),
            pltpu.VMEM(inverse.shape, bf16),
            blocks,
            pltpu.VMEM((pairs, rows, wide), bf16),
            pltpu.VMEM((m, pairs, rows, lanes), bf16),
            pltpu.VMEM((2, m * lanes, wide), bf16),
            pltpu.VMEM((n, 8, 128), f32),
            blocks,
            blocks,
            blocks,
            blocks,
            blocks,
            blocks,
            blocks,
            pltpu.VMEM((n, n, 8, rows), f32),
            pltpu.VMEM((n, 2 * rows, wide), f32),
            pltpu.VMEM((n, 2 * rows, wide), f32),
            pltpu.VMEM((n, wide // HD, rows, rows), f32),
            pltpu.VMEM((n, n, wide // HD, rows, rows), bf16),
            pltpu.VMEM((n, wide // HD, rows, HD), f32),
            dma((pairs,)),
            dma((pairs,)),
            dma((pairs, m)),
            dma((pairs, m)),
            dma((pairs,)),
            dma((pairs,)),
            dma((7, n)),
            dma((7, n)),
            dma((5,)),
            dma((8,)),
        ],
        compiler_params=pltpu.CompilerParams(
            collective_id=0, has_side_effects=True, vmem_limit_bytes=60 * 1024 * 1024
        ),
        name="hyena_attention",
    )(
        hyena_key, hyena_value, filters,
        groups.reshape(n, 1, wide), bias.reshape(n, 1, wide), block_mask,
        jnp.asarray(forward), jnp.asarray(inverse),
        hyena_query, att_queries, att_keys,
    )
    parts = 4
    return pl.pallas_call(
        functools.partial(copy_kernel, parts),
        out_shape=outs,
        in_specs=[anywhere] * 2,
        out_specs=[anywhere] * 2,
        scratch_shapes=[pltpu.VMEM((2, rows, channels), bf16), dma((2, parts)), dma((2, parts))],
        compiler_params=pltpu.CompilerParams(vmem_limit_bytes=60 * 1024 * 1024),
        name="results",
    )(hyena_out, attn_out)


def by_shape(
    n, m, hyena_query, hyena_key, hyena_value, bias, groups, filters, att_queries, att_keys, block_mask
):
    rows, channels = hyena_key.shape
    fits = (
        channels % (n * HD) == 0
        and n % 2 == 0
        and rows % (2 * ABLK) == 0
        and rows // ABLK <= 8
        and block_mask.shape[1] <= 128
        and filters.shape[0] % 128 == 0
        and filters.shape[1] == rows
    )
    args = (
        hyena_query, hyena_key, hyena_value, bias, groups, filters, att_queries, att_keys, block_mask
    )
    return fused_on_device(n, m, *args) if fits else on_device(*args)


def solution(mesh):
    return jax.shard_map(
        functools.partial(by_shape, mesh.shape["seq"], mesh.shape["chan"]),
        mesh=mesh,
        in_specs=(
            P("seq", "chan"),
            P("seq", "chan"),
            P("seq", "chan"),
            P("chan"),
            P("chan"),
            P("chan", "seq"),
            P("seq", "chan"),
            P("seq", "chan"),
            P("seq", None),
        ),
        out_specs=(P("seq", "chan"), P("seq", "chan")),
        check_vma=False,
    )
```
